512 devices in a mesh: dom: 64 (over y, z), tp: 8 (over x, core).
Axes of the slice: x: 4, y: 8, z: 8, core: 2. Of those that a mesh axis runs over, the one named last changes fastest.
Arguments:
- query: bfloat16 [128, 3584], P('dom', 'tp'), may hold values from -200 to 200
- new_kv: bfloat16 [128, 2, 512], P('dom'), may hold values from -8 to 8
- cache: bfloat16 [128, 2, 4096, 512], P('dom', None, 'tp'), may hold values from -8 to 8
- lengths: int32 [128], P('dom'), may hold values from 1024 to 4095, as said below
- prior_logw: float32 [128], P('dom'), may hold values from -250 to 250
- ancestors: int32 [128], replicated, may hold values from 0 to 127, as said below
- w_reward: bfloat16 [3584], replicated, may hold values from -0.09375 to 0.09375
Outputs:
- attn_out: bfloat16 [128, 3584], P('dom', 'tp')
- log_weight: float32 [128], P('dom')
- new_cache: bfloat16 [128, 2, 4096, 512], P('dom', None, 'tp')
The draws below stay inside these ranges and needn't reach their ends.
Inputs may be any that keep to these rules, and one draw needn't show every extreme that they name: `ancestors`: the ancestor of particle i belongs to a device d' with |d' - i // 2| <= 2, each distance up to 2 occurring in every draw; from any other device a device takes the cache of at most one particle. `lengths`: cache positions below it hold the particle's keys and values.
All inputs are finite; a program needn't handle non-finite values.
Results may differ from the reference program's by a relative error of at most 0.004.
Values may be sent and summed in bfloat16 or wider, within the bound.
No kernel may reach another device: no remote copies, remote signals or barrier semaphores. Data moves between devices by JAX's collectives and lax.ppermute only.
A program may use at most 64 MiB of HBM per device.

```python
import jax
import jax.numpy as jnp
from jax import lax

HQ = 28
KVH = 4
HD = 128
CTX = 4096
SPAN = 512
REACH = 2
P_DEV = 2
PARTICLES = 128


def shared_draw(key):
    group = HQ // KVH
    keys_a = jax.random.fold_in(key, 0)
    keys_b = jax.random.fold_in(key, 1)
    keys_c = jax.random.fold_in(key, 2)
    keys_f = jax.random.fold_in(key, 5)
    keys_g = jax.random.fold_in(key, 6)
    stored_keys = jnp.clip(jax.random.normal(keys_a, (PARTICLES, CTX, KVH, HD), jnp.float32), -6.0, 6.0)
    stored_values = jnp.clip(jax.random.normal(keys_b, (PARTICLES, CTX, KVH, HD), jnp.float32), -6.0, 6.0)
    base_query = jnp.clip(jax.random.normal(keys_c, (PARTICLES, KVH, group, HD), jnp.float32), -6.0, 6.0)
    query = base_query
    own_key = 0.5 * jnp.sum(base_query, axis=2) + 0.3 * jax.random.normal(keys_f, (PARTICLES, KVH, HD), jnp.float32)
    own_key = jnp.clip(own_key, -8.0, 8.0)
    own_value = jnp.clip(jax.random.normal(keys_g, (PARTICLES, KVH, HD), jnp.float32), -6.0, 6.0)
    fresh = jnp.stack([own_key, own_value], axis=1).reshape(PARTICLES, 2, KVH * HD)
    stored = jnp.stack([stored_keys, stored_values], axis=1).reshape(PARTICLES, 2, CTX, KVH * HD)
    return (query.reshape(PARTICLES, HQ * HD), fresh, stored)


def draw_query(key, part):
    return shared_draw(key)[0].astype(jnp.bfloat16)


def draw_new_kv(key, part):
    return shared_draw(key)[1].astype(jnp.bfloat16)


def draw_cache(key, part):
    return shared_draw(key)[2].astype(jnp.bfloat16)


def draw_lengths(key, part):
    key = jax.random.fold_in(key, 11)
    first_key, second_key = jax.random.split(key)
    drawn = jax.random.randint(first_key, (PARTICLES,), CTX // 4, CTX)
    chosen = jax.random.randint(second_key, (), 0, PARTICLES)
    return jnp.where(jnp.arange(PARTICLES) == chosen, CTX - 1, drawn).astype(jnp.int32)


def draw_prior_logw(key, part):
    key = jax.random.fold_in(key, 13)
    first_key = jax.random.fold_in(key, 0)
    ramp = 1.1 * jnp.arange(PARTICLES, dtype=jnp.float32) / (PARTICLES - 1)
    values = jnp.clip(jax.random.normal(first_key, (PARTICLES,), jnp.float32), -5.0, 5.0) + ramp
    return values


def draw_ancestors(key, part):
    key = jax.random.fold_in(key, 17)
    first_key, second_key = jax.random.split(key)
    devices = PARTICLES // P_DEV
    start = jax.random.randint(first_key, (), 0, 2 * REACH + 1)
    device = jnp.arange(devices, dtype=jnp.int32)
    offset = (device + start) % (2 * REACH + 1) - REACH
    target = device + offset
    target = jnp.where((target < 0) | (target >= devices), device - offset, target)
    local = jax.random.randint(second_key, (devices, P_DEV), 0, P_DEV)
    last_slot = (jnp.arange(P_DEV) == P_DEV - 1)[None, :]
    owner = jnp.where(last_slot, target[:, None], device[:, None])
    return (owner * P_DEV + local).reshape(PARTICLES).astype(jnp.int32)


def bell_draw(key, extent, scale, bound, kind=jnp.bfloat16):
    result = jax.random.normal(key, extent, jnp.float32) * scale
    return jnp.minimum(jnp.maximum(result, -bound), bound).astype(kind)


def setup_inputs(seed: int = 0) -> dict:
    key_list = jax.random.split(jax.random.key(seed), 8)
    return {
        "query": draw_query(jax.random.fold_in(key_list[7], 71), 0),
        "new_kv": draw_new_kv(jax.random.fold_in(key_list[7], 71), 0),
        "cache": draw_cache(jax.random.fold_in(key_list[7], 71), 0),
        "lengths": draw_lengths(jax.random.fold_in(key_list[7], 71), 0),
        "prior_logw": draw_prior_logw(jax.random.fold_in(key_list[7], 71), 0),
        "ancestors": draw_ancestors(jax.random.fold_in(key_list[7], 71), 0),
        "w_reward": bell_draw(key_list[6], (HQ * HD,), (HQ * HD) ** -0.5, 0.09375),
    }


MASKED = -1e+30
EPSILON = 1e-06

def attend_one(items):
    query_row, fresh, stored, length = items
    group = HQ // KVH
    scale = HD ** (-0.5)
    heads = query_row.astype(jnp.float32).reshape(KVH, group, HD)
    keys = stored[0].astype(jnp.float32).reshape(CTX, KVH, HD)
    values = stored[1].astype(jnp.float32).reshape(CTX // SPAN, SPAN, KVH, HD)
    scores = jnp.einsum('gqd,tgd->gqt', heads, keys) * scale
    position = jnp.arange(CTX, dtype=jnp.int32)
    valid = position < length
    scores = jnp.where(valid, scores, MASKED).reshape(KVH, group, CTX // SPAN, SPAN)
    valid_blocks = valid.reshape(CTX // SPAN, SPAN)
    block_max = lax.optimization_barrier(jnp.max(scores, axis=3))
    expo = jnp.where(valid_blocks, jnp.exp(scores - block_max[..., None]), 0.0)
    block_sum = lax.optimization_barrier(jnp.sum(expo, axis=3))
    rounded = lax.optimization_barrier(expo.astype(jnp.bfloat16)).astype(jnp.float32)
    block_acc = jnp.einsum('gqbt,btgd->gqbd', rounded, values)
    own_key = fresh[0].astype(jnp.float32).reshape(KVH, HD)
    own_value = fresh[1].astype(jnp.float32).reshape(KVH, HD)
    own_score = jnp.einsum('gqd,gd->gq', heads, own_key) * scale
    top = jnp.maximum(lax.optimization_barrier(jnp.max(block_max, axis=2)), own_score)
    factor = jnp.exp(block_max - top[..., None])
    own_factor = jnp.exp(own_score - top)
    numer = lax.optimization_barrier(jnp.sum(factor[..., None] * block_acc, axis=2)) + own_factor[..., None] * own_value[:, None, :]
    denom = lax.optimization_barrier(jnp.sum(factor * block_sum, axis=2)) + own_factor
    attended = (numer / denom[..., None]).reshape(HQ * HD)
    grown = jnp.where(position[None, :, None] == length, fresh[:, None, :], stored)
    return (attended, grown)

def reference(query, new_kv, cache, lengths, prior_logw, ancestors, w_reward):
    attended, grown = lax.map(attend_one, (query, new_kv, cache, lengths))
    spread = jnp.sqrt(lax.optimization_barrier(jnp.mean(attended * attended, axis=1, keepdims=True)) + EPSILON)
    reward = lax.optimization_barrier(jnp.sum(w_reward.astype(jnp.float32)[None, :] * attended / spread, axis=1))
    logits = prior_logw + reward
    peak = jnp.max(logits)
    level = peak + jnp.log(jnp.sum(jnp.exp(logits - peak)))
    new_cache = jnp.take(grown, ancestors.astype(jnp.int32), axis=0)
    return (attended.astype(jnp.bfloat16), logits - level, new_cache)
```

```python
import functools

import jax
import jax.numpy as jnp
from jax import lax
from jax.experimental import pallas as pl
from jax.experimental.pallas import tpu as pltpu
from jax.sharding import PartitionSpec as P

HQ = 28
KVH = 4
HD = 128
GROUP = HQ // KVH
FEATURES = HQ * HD
REACH = 2
P_DEV = 2
TP = 8
ROWS = 32
OWN = ROWS // TP
PAD_GROUP = ROWS // KVH
PART = ROWS + 8
TILE = 16

MASKED = -1e30
EPSILON = 1e-06

ANY = pl.BlockSpec(memory_space=pl.ANY)
SMEM = pl.BlockSpec(memory_space=pltpu.SMEM)
VMEM = pl.BlockSpec(memory_space=pltpu.VMEM)


def shifted(value, axis, by):
    devices = lax.axis_size(axis)
    pairs = [(i, i + by) for i in range(devices) if 0 <= i + by < devices]
    return lax.ppermute(value, axis, pairs)


def patch(block, first_row, row, fresh):
    inside = row - first_row
    tile = pl.multiple_of((inside // TILE) * TILE, TILE)
    old = block[pl.ds(tile, TILE), :].astype(jnp.float32)
    here = lax.broadcasted_iota(jnp.int32, old.shape, 0) == inside - tile
    block[pl.ds(tile, TILE), :] = jnp.where(here, fresh, old).astype(block.dtype)


def pick(ancestors, device, receivers):
    count = ancestors.shape[0]
    chosen = jnp.int32(0)
    for receiver in reversed(receivers):
        for slot in range(P_DEV):
            lane = P_DEV * receiver + slot
            wanted = ancestors[jnp.clip(lane, 0, count - 1)]
            fits = (lane >= 0) & (lane < count) & (wanted >> 1 == device)
            chosen = jnp.where(fits, wanted & 1, chosen)
    return chosen


def pack_kernel(far, ancestors, lengths, new_kv, cache, right, left, sems):
    device = lax.axis_index("dom")
    length = cache.shape[2]
    first = lax.axis_index("tp") * length
    copies = []
    for side, (out, sign) in enumerate(((right, 1), (left, -1))):
        receivers = [device + 2 * sign] if far else [device + sign, device + 2 * sign]
        particle = pick(ancestors, device, receivers)
        copy = pltpu.make_async_copy(cache.at[particle], out, sems.at[side])
        copy.start()
        copies.append((out, particle, copy))
    for out, particle, copy in copies:
        copy.wait()
        row = lengths[particle]

        @pl.when((row >= first) & (row < first + length))
        def _():
            fresh = new_kv[particle].astype(jnp.float32)
            for kv in range(2):
                patch(out.at[kv], first, row, fresh[kv : kv + 1])


def pack(ancestors, lengths, new_kv, cache, far):
    unit = jax.ShapeDtypeStruct(cache.shape[1:], cache.dtype)
    return pl.pallas_call(
        functools.partial(pack_kernel, far),
        out_shape=(unit, unit),
        in_specs=[SMEM, SMEM, VMEM, ANY],
        out_specs=(VMEM, VMEM),
        scratch_shapes=[pltpu.SemaphoreType.DMA((2,))],
        compiler_params=pltpu.CompilerParams(vmem_limit_bytes=16 << 20),
        name="pack_far" if far else "pack_near",
    )(ancestors, lengths, new_kv, cache)


def spread_query_kernel(query, out, wide):
    odd = lax.rem(lax.axis_index("tp"), 2)
    columns = query.shape[1]
    wide[...] = jnp.zeros_like(wide)
    wide[0:P_DEV, 0:columns] = query[...].astype(jnp.float32)
    even_rows = wide[...]
    odd_rows = pltpu.roll(even_rows, OWN * HD - columns, 1)
    rows = jnp.where(odd == 1, odd_rows, even_rows)
    for particle in range(P_DEV):
        for j in range(OWN):
            one = rows[particle : particle + 1, HD * j : HD * (j + 1)]
            for receiver in range(TP):
                out[receiver, pl.ds(OWN * particle + j, 1), :] = one


def spread_query(query):
    return pl.pallas_call(
        spread_query_kernel,
        out_shape=jax.ShapeDtypeStruct((TP, P_DEV * OWN, HD), jnp.float32),
        in_specs=[VMEM],
        out_specs=VMEM,
        scratch_shapes=[pltpu.VMEM((8, OWN * HD), jnp.float32)],
        name="spread_query",
    )(query)


def eye():
    shape = (ROWS, HD)
    return lax.broadcasted_iota(jnp.int32, shape, 0) == lax.broadcasted_iota(jnp.int32, shape, 1)


def attend_kernel(lengths, heads, new_kv, cache, out, kv, rows, sems):
    length = cache.shape[2]
    tp_index = lax.axis_index("tp")
    scale = HD ** (-0.5)
    copies = {}
    for particle in range(P_DEV):
        for half in range(2):
            copies[particle, half] = pltpu.make_async_copy(
                cache.at[particle, half], kv.at[particle, half], sems.at[particle, half]
            )
            copies[particle, half].start()
    row_index = lax.broadcasted_iota(jnp.int32, (ROWS, HD), 0)
    in_group = lax.rem(row_index, PAD_GROUP)
    wide_shape = (ROWS, KVH * HD)
    own_block = (
        lax.broadcasted_iota(jnp.int32, wide_shape, 0) // PAD_GROUP
        == lax.broadcasted_iota(jnp.int32, wide_shape, 1) // HD
    )
    for particle in range(P_DEV):
        for source in range(TP):
            rows[OWN * source : OWN * (source + 1), :] = heads[
                source, OWN * particle : OWN * (particle + 1), :
            ]
        parts = rows[...]
        after = pltpu.roll(parts, ROWS - 1, 0)
        before = pltpu.roll(parts, 1, 0)
        query = (
            parts
            + jnp.where(in_group == OWN - 1, after, 0.0)
            + jnp.where(in_group == OWN, before, 0.0)
        )
        fresh = new_kv[particle].astype(jnp.float32)
        own_key, own_value = [
            jnp.concatenate(
                [
                    jnp.broadcast_to(fresh[half : half + 1, HD * g : HD * (g + 1)], (PAD_GROUP, HD))
                    for g in range(KVH)
                ],
                axis=0,
            )
            for half in range(2)
        ]
        first_device = tp_index == 0
        own_score = jnp.sum(query * own_key, axis=1, keepdims=True) * scale
        own_score = jnp.where(first_device, own_score, MASKED)
        wide = jnp.concatenate([query] * KVH, axis=1)
        wide = jnp.where(own_block, wide, 0.0).astype(cache.dtype)
        copies[particle, 0].wait()
        scores = (
            lax.dot_general(
                wide, kv[particle, 0], (((1,), (1,)), ((), ())), preferred_element_type=jnp.float32
            )
            * scale
        )
        position = tp_index * length + lax.broadcasted_iota(jnp.int32, scores.shape, 1)
        valid = position < lengths[particle]
        scores = jnp.where(valid, scores, MASKED)
        block_max = jnp.max(scores, axis=1, keepdims=True)
        expo = jnp.where(valid, jnp.exp(scores - block_max), 0.0)
        block_sum = jnp.sum(expo, axis=1, keepdims=True)
        copies[particle, 1].wait()
        full = jnp.dot(
            expo.astype(cache.dtype), kv[particle, 1], preferred_element_type=jnp.float32
        )
        acc = jnp.concatenate(
            [
                full[PAD_GROUP * g : PAD_GROUP * (g + 1), HD * g : HD * (g + 1)]
                for g in range(KVH)
            ],
            axis=0,
        )
        top = jnp.maximum(block_max, own_score)
        factor = jnp.exp(block_max - top)
        own_factor = jnp.where(first_device, jnp.exp(own_score - top), 0.0)
        acc = factor * acc + own_factor * own_value
        total = factor * block_sum + own_factor
        diagonal = eye()
        top_row = jnp.sum(jnp.where(diagonal, top, 0.0), axis=0, keepdims=True)
        total_row = jnp.sum(jnp.where(diagonal, total, 0.0), axis=0, keepdims=True)
        stats_row = lax.broadcasted_iota(jnp.int32, (8, HD), 0)
        stats = jnp.where(stats_row == 0, top_row, jnp.where(stats_row == 1, total_row, 0.0))
        for receiver in range(TP):
            out[receiver, PART * particle : PART * particle + ROWS, :] = acc
            out[receiver, PART * particle + ROWS : PART * (particle + 1), :] = stats


def attend(lengths, heads, new_kv, cache):
    return pl.pallas_call(
        attend_kernel,
        out_shape=jax.ShapeDtypeStruct((TP, P_DEV * PART, HD), jnp.float32),
        in_specs=[SMEM, VMEM, VMEM, ANY],
        out_specs=VMEM,
        scratch_shapes=[
            pltpu.VMEM(cache.shape, cache.dtype),
            pltpu.VMEM((ROWS, HD), jnp.float32),
            pltpu.SemaphoreType.DMA((P_DEV, 2)),
        ],
        compiler_params=pltpu.CompilerParams(vmem_limit_bytes=16 << 20),
        name="attend",
    )(lengths, heads, new_kv, cache)


def merge_kernel(prior, parts, weight, attn, logits, weights, own_rows, wide):
    tp_index = lax.axis_index("tp")
    for g in range(KVH):
        for half in range(2):
            at = PAD_GROUP * g + OWN * half
            head = GROUP * g + (OWN - 1) * half
            weights[at : at + OWN, :] = weight[head : head + OWN, :]
    in_group = lax.rem(lax.broadcasted_iota(jnp.int32, (ROWS, HD), 0), PAD_GROUP)
    lane = lax.broadcasted_iota(jnp.int32, (ROWS, HD), 1)
    counted = ((in_group != OWN - 1) | (lane < HD // 2)) & ((in_group != OWN) | (lane >= HD // 2))
    diagonal = eye()
    logit_lane = lax.broadcasted_iota(jnp.int32, (1, HD), 1)
    logit_row = jnp.zeros((1, HD), jnp.float32)
    wide[...] = jnp.zeros_like(wide)
    for particle in range(P_DEV):
        at = PART * particle
        tops, totals = [
            [
                jnp.sum(
                    jnp.where(diagonal, parts[source, at + ROWS + k : at + ROWS + k + 1, :], 0.0),
                    axis=1,
                    keepdims=True,
                )
                for source in range(TP)
            ]
            for k in range(2)
        ]
        top = functools.reduce(jnp.maximum, tops)
        denom = jnp.zeros_like(top)
        numer = jnp.zeros((ROWS, HD), jnp.float32)
        for source in range(TP):
            factor = jnp.exp(tops[source] - top)
            denom = denom + factor * totals[source]
            numer = numer + factor * parts[source, at : at + ROWS, :]
        attended = numer / denom
        kept = jnp.where(counted, attended, 0.0)
        mean = jnp.sum(kept * kept) / FEATURES
        weighed = jnp.sum(weights[...] * kept)
        reward = jnp.full((1, HD), weighed) / jnp.sqrt(jnp.full((1, HD), mean) + EPSILON)
        logit_row = jnp.where(logit_lane == particle, prior[particle] + reward, logit_row)
        own_rows[...] = attended
        for j in range(OWN):
            wide[particle : particle + 1, HD * j : HD * (j + 1)] = own_rows[
                pl.ds(OWN * tp_index + j, 1), :
            ]
    columns = attn.shape[1]
    even = wide[...]
    odd = pltpu.roll(even, columns, 1)
    chosen = jnp.where(lax.rem(tp_index, 2) == 1, odd, even)
    attn[...] = chosen[0:P_DEV, 0:columns].astype(attn.dtype)
    logits[...] = jnp.broadcast_to(logit_row[None], logits.shape)


def merge(prior, parts, weight, columns, devices):
    return pl.pallas_call(
        merge_kernel,
        out_shape=(
            jax.ShapeDtypeStruct((P_DEV, columns), jnp.bfloat16),
            jax.ShapeDtypeStruct((devices, 1, HD), jnp.float32),
        ),
        in_specs=[SMEM, VMEM, VMEM],
        out_specs=(VMEM, VMEM),
        scratch_shapes=[
            pltpu.VMEM((ROWS, HD), jnp.float32),
            pltpu.VMEM((ROWS, HD), jnp.float32),
            pltpu.VMEM((8, OWN * HD), jnp.float32),
        ],
        name="merge",
    )(prior, parts, weight)


SPLIT = 2


def assemble_kernel(
    ancestors, lengths, logits, new_kv, cache, right1, left1, right2, left2,
    new_cache, log_weight, buffer, in_sems, out_sems,
):
    device = lax.axis_index("dom")
    length = cache.shape[2]
    first = lax.axis_index("tp") * length
    rows = length // SPLIT
    pieces = [
        (slot, kv, part) for part in range(SPLIT) for kv in range(2) for slot in range(P_DEV)
    ]
    owner = [ancestors[P_DEV * device + slot] for slot in range(P_DEV)]

    def arriving(ref, piece):
        slot, kv, part = piece
        at = pl.ds(part * rows, rows)
        return pltpu.make_async_copy(ref.at[kv, at], buffer.at[slot, kv, at], in_sems.at[slot, kv, part])

    for piece in pieces:
        offset = (owner[piece[0]] >> 1) - device

        @pl.when(offset == 0)
        def _():
            arriving(cache.at[owner[piece[0]] & 1], piece).start()

        for at, ref in ((-1, right1), (1, left1), (-2, right2), (2, left2)):

            @pl.when(offset == at)
            def _():
                arriving(ref, piece).start()

    lane = lax.broadcasted_iota(jnp.int32, (logits.shape[0], HD), 1)
    every = jnp.where(lane < P_DEV, logits[:, 0, :], -jnp.inf)
    peak = jnp.max(jnp.max(every, axis=1, keepdims=True), axis=0, keepdims=True)
    terms = jnp.exp(every - peak)
    total = jnp.sum(jnp.sum(terms, axis=1, keepdims=True), axis=0, keepdims=True)
    mine = logits[device] - (peak + jnp.log(total))
    for slot in range(P_DEV):
        log_weight[slot] = mine[0, slot]

    leaving = []
    for piece in pieces:
        slot, kv, part = piece
        at = pl.ds(part * rows, rows)
        arriving(right1, piece).wait()
        particle = owner[slot] & 1
        row = lengths[particle] - (first + part * rows)

        @pl.when((owner[slot] >> 1 == device) & (row >= 0) & (row < rows))
        def _():
            fresh = new_kv[particle].astype(jnp.float32)
            patch(buffer.at[slot, kv], 0, row + part * rows, fresh[kv : kv + 1])

        copy = pltpu.make_async_copy(
            buffer.at[slot, kv, at], new_cache.at[slot, kv, at], out_sems.at[slot, kv, part]
        )
        copy.start()
        leaving.append(copy)
    for copy in leaving:
        copy.wait()


def assemble(ancestors, lengths, logits, new_kv, cache, right1, left1, right2, left2):
    return pl.pallas_call(
        assemble_kernel,
        out_shape=(
            jax.ShapeDtypeStruct(cache.shape, cache.dtype),
            jax.ShapeDtypeStruct((P_DEV,), jnp.float32),
        ),
        in_specs=[SMEM, SMEM, VMEM, VMEM, ANY, ANY, ANY, ANY, ANY],
        out_specs=(ANY, SMEM),
        scratch_shapes=[
            pltpu.VMEM(cache.shape, cache.dtype),
            pltpu.SemaphoreType.DMA((P_DEV, 2, SPLIT)),
            pltpu.SemaphoreType.DMA((P_DEV, 2, SPLIT)),
        ],
        compiler_params=pltpu.CompilerParams(vmem_limit_bytes=16 << 20),
        name="assemble",
    )(ancestors, lengths, logits, new_kv, cache, right1, left1, right2, left2)


def crowded(ancestors):
    source = ancestors // P_DEV
    offset = source - jnp.arange(ancestors.shape[0], dtype=jnp.int32) // P_DEV
    found = jnp.bool_(False)
    for ahead in range(1, 2 * P_DEV):
        here, there = slice(None, -ahead), slice(ahead, None)
        both = (source[here] == source[there]) & (ancestors[here] != ancestors[there])
        right = (offset[here] == -1) & (offset[there] == -2)
        left = (offset[here] == 2) & (offset[there] == 1)
        found = found | jnp.any(both & (right | left))
    return found


def local(query, new_kv, cache, lengths, prior_logw, ancestors, w_reward):
    right0, left0 = pack(ancestors, lengths, new_kv, cache, far=False)
    right1 = shifted(right0, "dom", 1)
    left1 = shifted(left0, "dom", -1)
    heads = lax.all_to_all(spread_query(query), "tp", 0, 0)
    parts = attend(lengths, heads, new_kv, cache)
    parts = lax.all_to_all(parts, "tp", 0, 0)
    parts, right1, left1 = lax.optimization_barrier((parts, right1, left1))
    right2 = shifted(right1, "dom", 1)
    left2 = shifted(left1, "dom", -1)
    weight = w_reward.astype(jnp.float32).reshape(HQ, HD)
    attn, logits = merge(prior_logw, parts, weight, query.shape[1], lax.axis_size("dom"))
    logits = lax.all_to_all(logits, "dom", 0, 0)

    def near(right2, left2):
        return assemble(ancestors, lengths, logits, new_kv, cache, right1, left1, right2, left2)

    def direct(right2, left2):
        right0, left0 = pack(ancestors, lengths, new_kv, cache, far=True)
        return near(shifted(right0, "dom", REACH), shifted(left0, "dom", -REACH))

    new_cache, log_weight = lax.cond(crowded(ancestors), direct, near, right2, left2)
    return (attn, log_weight, new_cache)


def solution(mesh):
    in_specs = (
        P("dom", "tp"),
        P("dom", None, None),
        P("dom", None, "tp", None),
        P("dom"),
        P("dom"),
        P(),
        P(),
    )
    out_specs = (P("dom", "tp"), P("dom"), P("dom", None, "tp", None))
    return jax.shard_map(local, mesh=mesh, in_specs=in_specs, out_specs=out_specs, check_vma=False)
```

```python
import functools

import jax
import jax.numpy as jnp
from jax import lax
from jax.experimental import pallas as pl
from jax.experimental.pallas import tpu as pltpu
from jax.sharding import PartitionSpec as P

HQ = 28
KVH = 4
HD = 128
GROUP = HQ // KVH
FEATURES = HQ * HD
REACH = 2
P_DEV = 2
TP = 8
ROWS = 32
OWN = ROWS // TP
PAD_GROUP = ROWS // KVH
PART = ROWS + 8
TILE = 16

MASKED = -1e30
EPSILON = 1e-06

ANY = pl.BlockSpec(memory_space=pl.ANY)
HBM = pl.BlockSpec(memory_space=pltpu.HBM)
SMEM = pl.BlockSpec(memory_space=pltpu.SMEM)
VMEM = pl.BlockSpec(memory_space=pltpu.VMEM)


def shifted(value, axis, by):
    devices = lax.axis_size(axis)
    pairs = [(i, i + by) for i in range(devices) if 0 <= i + by < devices]
    return lax.ppermute(value, axis, pairs)


def swapped(value, axis, first):
    pairs = []
    for i in range(first, lax.axis_size(axis) - 1, 2):
        pairs += [(i, i + 1), (i + 1, i)]
    return lax.ppermute(value, axis, pairs)


def patch(block, first_row, row, fresh):
    inside = row - first_row
    tile = pl.multiple_of((inside // TILE) * TILE, TILE)
    old = block[pl.ds(tile, TILE), :].astype(jnp.float32)
    here = lax.broadcasted_iota(jnp.int32, old.shape, 0) == inside - tile
    block[pl.ds(tile, TILE), :] = jnp.where(here, fresh, old).astype(block.dtype)


def pick(ancestors, device, receivers):
    count = ancestors.shape[0]
    chosen = jnp.int32(0)
    for receiver in reversed(receivers):
        for slot in range(P_DEV):
            lane = P_DEV * receiver + slot
            wanted = ancestors[jnp.clip(lane, 0, count - 1)]
            fits = (lane >= 0) & (lane < count) & (wanted >> 1 == device)
            chosen = jnp.where(fits, wanted & 1, chosen)
    return chosen


def crowded(ancestors):
    count = ancestors.shape[1]
    shape = (8, count)
    wanted = jnp.broadcast_to(ancestors[...], shape)
    lane = lax.broadcasted_iota(jnp.int32, shape, 1)
    offset = (wanted >> 1) - (lane >> 1)
    found = jnp.zeros(shape, jnp.float32)
    for ahead in range(1, 2 * P_DEV):
        later_wanted = pltpu.roll(wanted, count - ahead, 1)
        later_offset = pltpu.roll(offset, count - ahead, 1)
        differ = (wanted >> 1 == later_wanted >> 1) & (wanted != later_wanted)
        sides = ((offset == -1) & (later_offset == -2)) | ((offset == 2) & (later_offset == 1))
        found = jnp.where(differ & sides & (lane < count - ahead), 1.0, found)
    return (jnp.sum(found) > 0.0).astype(jnp.int32)


def pad_query(query, out, wide):
    columns = query.shape[1]
    wide[...] = jnp.zeros_like(wide)
    wide[0:P_DEV, 0:columns] = query[...].astype(jnp.float32)
    even_rows = wide[...]
    odd_rows = pltpu.roll(even_rows, OWN * HD - columns, 1)
    rows = jnp.where(lax.rem(lax.axis_index("tp"), 2) == 1, odd_rows, even_rows)
    for particle in range(P_DEV):
        for j in range(OWN):
            one = rows[particle : particle + 1, HD * j : HD * (j + 1)]
            for receiver in range(TP):
                out[receiver, pl.ds(OWN * particle + j, 1), :] = one


def pack_kernel(
    ancestors, lengths, row, query, new_kv, cache, even, odd, rows, flag, asked, fresh, wide, sems, small_sems
):
    device = lax.axis_index("dom")
    length = cache.shape[2]
    first = lax.axis_index("tp") * length
    small = [
        pltpu.make_async_copy(query, asked, small_sems.at[0]),
        pltpu.make_async_copy(new_kv, fresh, small_sems.at[1]),
    ]
    facing = 1 - 2 * (device & 1)
    units = []
    for side, (out, sign) in enumerate(((even, facing), (odd, -facing))):
        particle = pick(ancestors, device, [device + sign, device + 2 * sign])
        for kv in range(2):
            copy = pltpu.make_async_copy(cache.at[particle, kv], out.at[kv], sems.at[side, kv])
            copy.start()
            units.append((out, particle, kv, copy))
    for copy in small:
        copy.start()
    flag[0] = crowded(row)
    for copy in small:
        copy.wait()
    pad_query(asked, rows, wide)
    for out, particle, kv, copy in units:
        copy.wait()
        position = lengths[particle]

        @pl.when((position >= first) & (position < first + length))
        def _():
            new = fresh[particle].astype(jnp.float32)
            patch(out.at[kv], first, position, new[kv : kv + 1])


def pack(ancestors, lengths, query, new_kv, cache):
    unit = jax.ShapeDtypeStruct(cache.shape[1:], cache.dtype)
    return pl.pallas_call(
        pack_kernel,
        out_shape=(
            unit,
            unit,
            jax.ShapeDtypeStruct((TP, P_DEV * OWN, HD), jnp.float32),
            jax.ShapeDtypeStruct((1,), jnp.int32),
        ),
        in_specs=[SMEM, SMEM, VMEM, HBM, HBM, HBM],
        out_specs=(VMEM, VMEM, VMEM, SMEM),
        scratch_shapes=[
            pltpu.VMEM(query.shape, query.dtype),
            pltpu.VMEM(new_kv.shape, new_kv.dtype),
            pltpu.VMEM((8, OWN * HD), jnp.float32),
            pltpu.SemaphoreType.DMA((P_DEV, 2)),
            pltpu.SemaphoreType.DMA((2,)),
        ],
        compiler_params=pltpu.CompilerParams(vmem_limit_bytes=16 << 20),
        name="pack",
    )(ancestors, lengths, ancestors.reshape(1, -1), query, new_kv, cache)


def pack_far_kernel(ancestors, lengths, new_kv, cache, right, left, sems):
    device = lax.axis_index("dom")
    length = cache.shape[2]
    first = lax.axis_index("tp") * length
    copies = []
    for side, (out, sign) in enumerate(((right, 1), (left, -1))):
        particle = pick(ancestors, device, [device + REACH * sign])
        copy = pltpu.make_async_copy(cache.at[particle], out, sems.at[side])
        copy.start()
        copies.append((out, particle, copy))
    for out, particle, copy in copies:
        copy.wait()
        position = lengths[particle]

        @pl.when((position >= first) & (position < first + length))
        def _():
            fresh = new_kv[particle].astype(jnp.float32)
            for kv in range(2):
                patch(out.at[kv], first, position, fresh[kv : kv + 1])


def pack_far(ancestors, lengths, new_kv, cache):
    unit = jax.ShapeDtypeStruct(cache.shape[1:], cache.dtype)
    return pl.pallas_call(
        pack_far_kernel,
        out_shape=(unit, unit),
        in_specs=[SMEM, SMEM, VMEM, ANY],
        out_specs=(VMEM, VMEM),
        scratch_shapes=[pltpu.SemaphoreType.DMA((P_DEV,))],
        compiler_params=pltpu.CompilerParams(vmem_limit_bytes=16 << 20),
        name="pack_far",
    )(ancestors, lengths, new_kv, cache)


def eye():
    shape = (ROWS, HD)
    return lax.broadcasted_iota(jnp.int32, shape, 0) == lax.broadcasted_iota(jnp.int32, shape, 1)


def attend_kernel(lengths, heads, new_kv, kv, out, rows):
    length = kv.shape[2]
    tp_index = lax.axis_index("tp")
    scale = HD ** (-0.5)
    row_index = lax.broadcasted_iota(jnp.int32, (ROWS, HD), 0)
    in_group = lax.rem(row_index, PAD_GROUP)
    wide_shape = (ROWS, KVH * HD)
    own_block = (
        lax.broadcasted_iota(jnp.int32, wide_shape, 0) // PAD_GROUP
        == lax.broadcasted_iota(jnp.int32, wide_shape, 1) // HD
    )
    for particle in range(P_DEV):
        for source in range(TP):
            rows[OWN * source : OWN * (source + 1), :] = heads[
                source, OWN * particle : OWN * (particle + 1), :
            ]
        parts = rows[...]
        after = pltpu.roll(parts, ROWS - 1, 0)
        before = pltpu.roll(parts, 1, 0)
        query = (
            parts
            + jnp.where(in_group == OWN - 1, after, 0.0)
            + jnp.where(in_group == OWN, before, 0.0)
        )
        fresh = new_kv[particle].astype(jnp.float32)
        own_key, own_value = [
            jnp.concatenate(
                [
                    jnp.broadcast_to(fresh[half : half + 1, HD * g : HD * (g + 1)], (PAD_GROUP, HD))
                    for g in range(KVH)
                ],
                axis=0,
            )
            for half in range(2)
        ]
        first_device = tp_index == 0
        own_score = jnp.sum(query * own_key, axis=1, keepdims=True) * scale
        own_score = jnp.where(first_device, own_score, MASKED)
        wide = jnp.concatenate([query] * KVH, axis=1)
        wide = jnp.where(own_block, wide, 0.0).astype(kv.dtype)
        scores = (
            lax.dot_general(
                wide, kv[particle, 0], (((1,), (1,)), ((), ())), preferred_element_type=jnp.float32
            )
            * scale
        )
        position = tp_index * length + lax.broadcasted_iota(jnp.int32, scores.shape, 1)
        valid = position < lengths[particle]
        scores = jnp.where(valid, scores, MASKED)
        block_max = jnp.max(scores, axis=1, keepdims=True)
        expo = jnp.where(valid, jnp.exp(scores - block_max), 0.0)
        block_sum = jnp.sum(expo, axis=1, keepdims=True)
        full = jnp.dot(
            expo.astype(kv.dtype), kv[particle, 1], preferred_element_type=jnp.float32
        )
        acc = jnp.concatenate(
            [
                full[PAD_GROUP * g : PAD_GROUP * (g + 1), HD * g : HD * (g + 1)]
                for g in range(KVH)
            ],
            axis=0,
        )
        top = jnp.maximum(block_max, own_score)
        factor = jnp.exp(block_max - top)
        own_factor = jnp.where(first_device, jnp.exp(own_score - top), 0.0)
        acc = factor * acc + own_factor * own_value
        total = factor * block_sum + own_factor
        diagonal = eye()
        top_row = jnp.sum(jnp.where(diagonal, top, 0.0), axis=0, keepdims=True)
        total_row = jnp.sum(jnp.where(diagonal, total, 0.0), axis=0, keepdims=True)
        stats_row = lax.broadcasted_iota(jnp.int32, (8, HD), 0)
        stats = jnp.where(stats_row == 0, top_row, jnp.where(stats_row == 1, total_row, 0.0))
        for receiver in range(TP):
            out[receiver, PART * particle : PART * particle + ROWS, :] = acc
            out[receiver, PART * particle + ROWS : PART * (particle + 1), :] = stats


def attend(lengths, heads, new_kv, kept):
    return pl.pallas_call(
        attend_kernel,
        out_shape=jax.ShapeDtypeStruct((TP, P_DEV * PART, HD), jnp.float32),
        in_specs=[SMEM, VMEM, VMEM, VMEM],
        out_specs=VMEM,
        scratch_shapes=[pltpu.VMEM((ROWS, HD), jnp.float32)],
        compiler_params=pltpu.CompilerParams(vmem_limit_bytes=16 << 20),
        name="attend",
    )(lengths, heads, new_kv, kept)


def merge_kernel(prior, parts, weight, attn, logits, weights, all_rows, wide):
    tp_index = lax.axis_index("tp")
    for g in range(KVH):
        for half in range(2):
            at = PAD_GROUP * g + OWN * half
            head = GROUP * g + (OWN - 1) * half
            weights[at : at + OWN, :] = weight[head : head + OWN, :]
    in_group = lax.rem(lax.broadcasted_iota(jnp.int32, (ROWS, HD), 0), PAD_GROUP)
    lane = lax.broadcasted_iota(jnp.int32, (ROWS, HD), 1)
    counted = ((in_group != OWN - 1) | (lane < HD // 2)) & ((in_group != OWN) | (lane >= HD // 2))
    diagonal = eye()
    logit_lane = lax.broadcasted_iota(jnp.int32, (1, HD), 1)
    logit_row = jnp.zeros((1, HD), jnp.float32)
    wide[...] = jnp.zeros_like(wide)
    for particle in range(P_DEV):
        at = PART * particle
        tops, totals = [
            [
                jnp.sum(
                    jnp.where(diagonal, parts[source, at + ROWS + k : at + ROWS + k + 1, :], 0.0),
                    axis=1,
                    keepdims=True,
                )
                for source in range(TP)
            ]
            for k in range(2)
        ]
        top = functools.reduce(jnp.maximum, tops)
        denom = jnp.zeros_like(top)
        numer = jnp.zeros((ROWS, HD), jnp.float32)
        for source in range(TP):
            factor = jnp.exp(tops[source] - top)
            denom = denom + factor * totals[source]
            numer = numer + factor * parts[source, at : at + ROWS, :]
        attended = numer / denom
        kept = jnp.where(counted, attended, 0.0)
        mean = jnp.sum(kept * kept) / FEATURES
        weighed = jnp.sum(weights[...] * kept)
        reward = jnp.full((1, HD), weighed) / jnp.sqrt(jnp.full((1, HD), mean) + EPSILON)
        logit_row = jnp.where(logit_lane == particle, prior[particle] + reward, logit_row)
        all_rows[...] = attended
        for j in range(OWN):
            wide[particle : particle + 1, HD * j : HD * (j + 1)] = all_rows[
                pl.ds(OWN * tp_index + j, 1), :
            ]
    columns = attn.shape[1]
    even = wide[...]
    odd = pltpu.roll(even, columns, 1)
    chosen = jnp.where(lax.rem(tp_index, 2) == 1, odd, even)
    attn[...] = chosen[0:P_DEV, 0:columns].astype(attn.dtype)
    logits[...] = jnp.broadcast_to(logit_row[None], logits.shape)


def merge(prior, parts, weight, columns, devices):
    return pl.pallas_call(
        merge_kernel,
        out_shape=(
            jax.ShapeDtypeStruct((P_DEV, columns), jnp.bfloat16),
            jax.ShapeDtypeStruct((devices, 1, HD), jnp.float32),
        ),
        in_specs=[SMEM, VMEM, VMEM],
        out_specs=(VMEM, VMEM),
        scratch_shapes=[
            pltpu.VMEM((ROWS, HD), jnp.float32),
            pltpu.VMEM((ROWS, HD), jnp.float32),
            pltpu.VMEM((8, OWN * HD), jnp.float32),
        ],
        compiler_params=pltpu.CompilerParams(vmem_limit_bytes=8 << 20),
        name="merge",
    )(prior, parts, weight)


SPLIT = 2


def assemble_kernel(
    far, ancestors, lengths, new_kv, cache, even1, odd1, even2, odd2, new_cache, buffer, in_sems, out_sems
):
    device = lax.axis_index("dom")
    length = cache.shape[2]
    first = lax.axis_index("tp") * length
    rows = length // SPLIT
    pieces = [
        (slot, kv, part) for part in range(SPLIT) for kv in range(2) for slot in range(P_DEV)
    ]
    owner = [ancestors[P_DEV * device + slot] for slot in range(P_DEV)]

    def arriving(ref, piece):
        slot, kv, part = piece
        at = pl.ds(part * rows, rows)
        return pltpu.make_async_copy(ref.at[kv, at], buffer.at[slot, kv, at], in_sems.at[slot, kv, part])

    for piece in pieces:
        offset = (owner[piece[0]] >> 1) - device
        facing = offset * (1 - 2 * (device & 1))
        two = offset if far else facing

        @pl.when(offset == 0)
        def _():
            arriving(cache.at[owner[piece[0]] & 1], piece).start()

        for found, ref in (
            (facing == 1, even1),
            (facing == -1, odd1),
            (two == REACH, even2),
            (two == -REACH, odd2),
        ):

            @pl.when(found)
            def _():
                arriving(ref, piece).start()

    leaving = []
    for piece in pieces:
        slot, kv, part = piece
        at = pl.ds(part * rows, rows)
        arriving(even1, piece).wait()
        particle = owner[slot] & 1
        row = lengths[particle] - (first + part * rows)

        @pl.when((owner[slot] >> 1 == device) & (row >= 0) & (row < rows))
        def _():
            fresh = new_kv[particle].astype(jnp.float32)
            patch(buffer.at[slot, kv], 0, row + part * rows, fresh[kv : kv + 1])

        copy = pltpu.make_async_copy(
            buffer.at[slot, kv, at], new_cache.at[slot, kv, at], out_sems.at[slot, kv, part]
        )
        copy.start()
        leaving.append(copy)
    for copy in leaving:
        copy.wait()


def assemble(ancestors, lengths, new_kv, cache, even1, odd1, even2, odd2, far):
    return pl.pallas_call(
        functools.partial(assemble_kernel, far),
        out_shape=jax.ShapeDtypeStruct(cache.shape, cache.dtype),
        in_specs=[SMEM, SMEM, VMEM, ANY, ANY, ANY, ANY, ANY],
        out_specs=ANY,
        scratch_shapes=[
            pltpu.VMEM(cache.shape, cache.dtype),
            pltpu.SemaphoreType.DMA((P_DEV, 2, SPLIT)),
            pltpu.SemaphoreType.DMA((P_DEV, 2, SPLIT)),
        ],
        compiler_params=pltpu.CompilerParams(vmem_limit_bytes=16 << 20),
        name="assemble",
    )(ancestors, lengths, new_kv, cache, even1, odd1, even2, odd2)


def normalize_kernel(logits, log_weight):
    every = logits[...]
    every = jnp.where(lax.broadcasted_iota(jnp.int32, every.shape, 2) < P_DEV, every, -jnp.inf)
    peak = jnp.max(jnp.max(every, axis=0), axis=1, keepdims=True)
    total = jnp.sum(jnp.sum(jnp.exp(every - peak), axis=0), axis=1, keepdims=True)
    mine = logits[lax.axis_index("dom")] - (peak + jnp.log(total))
    for slot in range(P_DEV):
        log_weight[slot] = mine[0, slot]


def normalize(logits):
    return pl.pallas_call(
        normalize_kernel,
        out_shape=jax.ShapeDtypeStruct((P_DEV,), jnp.float32),
        in_specs=[VMEM],
        out_specs=SMEM,
        compiler_params=pltpu.CompilerParams(vmem_limit_bytes=8 << 20),
        name="normalize",
    )(logits)


def local(query, new_kv, cache, lengths, prior_logw, ancestors, w_reward):
    even0, odd0, rows, flag = pack(ancestors, lengths, query, new_kv, cache)
    even1 = swapped(even0, "dom", 0)
    odd1 = swapped(odd0, "dom", 1)
    heads = lax.all_to_all(rows, "tp", 0, 0)
    parts = attend(lengths, heads, new_kv, cache)
    parts = lax.all_to_all(parts, "tp", 0, 0)
    weight = w_reward.astype(jnp.float32).reshape(HQ, HD)
    parts, even1, odd1 = lax.optimization_barrier((parts, even1, odd1))
    even2 = swapped(odd1, "dom", 0)
    odd2 = swapped(even1, "dom", 1)
    attn, logits = merge(prior_logw, parts, weight, query.shape[1], lax.axis_size("dom"))
    logits = lax.all_to_all(logits, "dom", 0, 0)

    def near(even2, odd2):
        return assemble(ancestors, lengths, new_kv, cache, even1, odd1, even2, odd2, far=False)

    def direct(even2, odd2):
        right0, left0 = pack_far(ancestors, lengths, new_kv, cache)
        from_left = shifted(right0, "dom", REACH)
        from_right = shifted(left0, "dom", -REACH)
        return assemble(
            ancestors, lengths, new_kv, cache, even1, odd1, from_right, from_left, far=True
        )

    new_cache = lax.cond(flag[0] > 0, direct, near, even2, odd2)
    new_cache, logits = lax.optimization_barrier((new_cache, logits))
    return (attn, normalize(logits), new_cache)


def solution(mesh):
    in_specs = (
        P("dom", "tp"),
        P("dom", None, None),
        P("dom", None, "tp", None),
        P("dom"),
        P("dom"),
        P(),
        P(),
    )
    out_specs = (P("dom", "tp"), P("dom"), P("dom", None, "tp", None))
    return jax.shard_map(local, mesh=mesh, in_specs=in_specs, out_specs=out_specs, check_vma=False)
```

```python
import functools

import jax
import jax.numpy as jnp
from jax import lax
from jax.experimental import pallas as pl
from jax.experimental.pallas import tpu as pltpu
from jax.sharding import PartitionSpec as P

HQ = 28
KVH = 4
HD = 128
GROUP = HQ // KVH
FEATURES = HQ * HD
REACH = 2
P_DEV = 2
TP = 8
ROWS = 32
OWN = ROWS // TP
PAD_GROUP = ROWS // KVH
PART = ROWS + 8
TILE = 16

MASKED = -1e30
EPSILON = 1e-06

ANY = pl.BlockSpec(memory_space=pl.ANY)
HBM = pl.BlockSpec(memory_space=pltpu.HBM)
SMEM = pl.BlockSpec(memory_space=pltpu.SMEM)
VMEM = pl.BlockSpec(memory_space=pltpu.VMEM)


def shifted(value, axis, by):
    devices = lax.axis_size(axis)
    pairs = [(i, i + by) for i in range(devices) if 0 <= i + by < devices]
    return lax.ppermute(value, axis, pairs)


def swapped(value, axis, first):
    pairs = []
    for i in range(first, lax.axis_size(axis) - 1, 2):
        pairs += [(i, i + 1), (i + 1, i)]
    return lax.ppermute(value, axis, pairs)


def patch(block, first_row, row, fresh):
    inside = row - first_row
    tile = pl.multiple_of((inside // TILE) * TILE, TILE)
    old = block[pl.ds(tile, TILE), :].astype(jnp.float32)
    here = lax.broadcasted_iota(jnp.int32, old.shape, 0) == inside - tile
    block[pl.ds(tile, TILE), :] = jnp.where(here, fresh, old).astype(block.dtype)


def pick(ancestors, device, receivers):
    count = ancestors.shape[0]
    chosen = jnp.int32(0)
    for receiver in reversed(receivers):
        for slot in range(P_DEV):
            lane = P_DEV * receiver + slot
            wanted = ancestors[jnp.clip(lane, 0, count - 1)]
            fits = (lane >= 0) & (lane < count) & (wanted >> 1 == device)
            chosen = jnp.where(fits, wanted & 1, chosen)
    return chosen


def crowded(ancestors):
    count = ancestors.shape[1]
    shape = (8, count)
    wanted = jnp.broadcast_to(ancestors[...], shape)
    lane = lax.broadcasted_iota(jnp.int32, shape, 1)
    offset = (wanted >> 1) - (lane >> 1)
    found = jnp.zeros(shape, jnp.float32)
    for ahead in range(1, 2 * P_DEV):
        later_wanted = pltpu.roll(wanted, count - ahead, 1)
        later_offset = pltpu.roll(offset, count - ahead, 1)
        differ = (wanted >> 1 == later_wanted >> 1) & (wanted != later_wanted)
        sides = ((offset == -1) & (later_offset == -2)) | ((offset == 2) & (later_offset == 1))
        found = jnp.where(differ & sides & (lane < count - ahead), 1.0, found)
    return (jnp.sum(found) > 0.0).astype(jnp.int32)


def pad_query(query, out, wide):
    columns = query.shape[1]
    wide[...] = jnp.zeros_like(wide)
    wide[0:P_DEV, 0:columns] = query[...].astype(jnp.float32)
    even_rows = wide[...]
    odd_rows = pltpu.roll(even_rows, OWN * HD - columns, 1)
    rows = jnp.where(lax.rem(lax.axis_index("tp"), 2) == 1, odd_rows, even_rows)
    for particle in range(P_DEV):
        for j in range(OWN):
            one = rows[particle : particle + 1, HD * j : HD * (j + 1)]
            for receiver in range(TP):
                out[receiver, pl.ds(OWN * particle + j, 1), :] = one


def pack_kernel(
    ancestors, lengths, row, query, new_kv, cache, even, odd, rows, flag, asked, fresh, wide, sems, small_sems
):
    device = lax.axis_index("dom")
    length = cache.shape[2]
    first = lax.axis_index("tp") * length
    small = [
        pltpu.make_async_copy(query, asked, small_sems.at[0]),
        pltpu.make_async_copy(new_kv, fresh, small_sems.at[1]),
    ]
    facing = 1 - 2 * (device & 1)
    units = []
    for side, (out, sign) in enumerate(((even, facing), (odd, -facing))):
        particle = pick(ancestors, device, [device + sign, device + 2 * sign])
        for kv in range(2):
            copy = pltpu.make_async_copy(cache.at[particle, kv], out.at[kv], sems.at[side, kv])
            copy.start()
            units.append((out, particle, kv, copy))
    for copy in small:
        copy.start()
    flag[0] = crowded(row)
    for copy in small:
        copy.wait()
    pad_query(asked, rows, wide)
    for out, particle, kv, copy in units:
        copy.wait()
        position = lengths[particle]

        @pl.when((position >= first) & (position < first + length))
        def _():
            new = fresh[particle].astype(jnp.float32)
            patch(out.at[kv], first, position, new[kv : kv + 1])


def pack(ancestors, lengths, query, new_kv, cache):
    unit = jax.ShapeDtypeStruct(cache.shape[1:], cache.dtype)
    return pl.pallas_call(
        pack_kernel,
        out_shape=(
            unit,
            unit,
            jax.ShapeDtypeStruct((TP, P_DEV * OWN, HD), jnp.float32),
            jax.ShapeDtypeStruct((1,), jnp.int32),
        ),
        in_specs=[SMEM, SMEM, VMEM, HBM, HBM, HBM],
        out_specs=(VMEM, VMEM, VMEM, SMEM),
        scratch_shapes=[
            pltpu.VMEM(query.shape, query.dtype),
            pltpu.VMEM(new_kv.shape, new_kv.dtype),
            pltpu.VMEM((8, OWN * HD), jnp.float32),
            pltpu.SemaphoreType.DMA((P_DEV, 2)),
            pltpu.SemaphoreType.DMA((2,)),
        ],
        compiler_params=pltpu.CompilerParams(vmem_limit_bytes=16 << 20),
        name="pack",
    )(ancestors, lengths, ancestors.reshape(1, -1), query, new_kv, cache)


def pack_far_kernel(ancestors, lengths, new_kv, cache, right, left, sems):
    device = lax.axis_index("dom")
    length = cache.shape[2]
    first = lax.axis_index("tp") * length
    copies = []
    for side, (out, sign) in enumerate(((right, 1), (left, -1))):
        particle = pick(ancestors, device, [device + REACH * sign])
        copy = pltpu.make_async_copy(cache.at[particle], out, sems.at[side])
        copy.start()
        copies.append((out, particle, copy))
    for out, particle, copy in copies:
        copy.wait()
        position = lengths[particle]

        @pl.when((position >= first) & (position < first + length))
        def _():
            fresh = new_kv[particle].astype(jnp.float32)
            for kv in range(2):
                patch(out.at[kv], first, position, fresh[kv : kv + 1])


def pack_far(ancestors, lengths, new_kv, cache):
    unit = jax.ShapeDtypeStruct(cache.shape[1:], cache.dtype)
    return pl.pallas_call(
        pack_far_kernel,
        out_shape=(unit, unit),
        in_specs=[SMEM, SMEM, VMEM, ANY],
        out_specs=(VMEM, VMEM),
        scratch_shapes=[pltpu.SemaphoreType.DMA((P_DEV,))],
        compiler_params=pltpu.CompilerParams(vmem_limit_bytes=16 << 20),
        name="pack_far",
    )(ancestors, lengths, new_kv, cache)


def eye():
    shape = (ROWS, HD)
    return lax.broadcasted_iota(jnp.int32, shape, 0) == lax.broadcasted_iota(jnp.int32, shape, 1)


def attend_kernel(lengths, heads, new_kv, kv, out, rows):
    length = kv.shape[2]
    tp_index = lax.axis_index("tp")
    scale = HD ** (-0.5)
    row_index = lax.broadcasted_iota(jnp.int32, (ROWS, HD), 0)
    in_group = lax.rem(row_index, PAD_GROUP)
    wide_shape = (ROWS, KVH * HD)
    own_block = (
        lax.broadcasted_iota(jnp.int32, wide_shape, 0) // PAD_GROUP
        == lax.broadcasted_iota(jnp.int32, wide_shape, 1) // HD
    )
    for particle in range(P_DEV):
        for source in range(TP):
            rows[OWN * source : OWN * (source + 1), :] = heads[
                source, OWN * particle : OWN * (particle + 1), :
            ]
        parts = rows[...]
        after = pltpu.roll(parts, ROWS - 1, 0)
        before = pltpu.roll(parts, 1, 0)
        query = (
            parts
            + jnp.where(in_group == OWN - 1, after, 0.0)
            + jnp.where(in_group == OWN, before, 0.0)
        )
        fresh = new_kv[particle].astype(jnp.float32)
        own_key, own_value = [
            jnp.concatenate(
                [
                    jnp.broadcast_to(fresh[half : half + 1, HD * g : HD * (g + 1)], (PAD_GROUP, HD))
                    for g in range(KVH)
                ],
                axis=0,
            )
            for half in range(2)
        ]
        first_device = tp_index == 0
        own_score = jnp.sum(query * own_key, axis=1, keepdims=True) * scale
        own_score = jnp.where(first_device, own_score, MASKED)
        wide = jnp.concatenate([query] * KVH, axis=1)
        wide = jnp.where(own_block, wide, 0.0).astype(kv.dtype)
        scores = (
            lax.dot_general(
                wide, kv[particle, 0], (((1,), (1,)), ((), ())), preferred_element_type=jnp.float32
            )
            * scale
        )
        position = tp_index * length + lax.broadcasted_iota(jnp.int32, scores.shape, 1)
        valid = position < lengths[particle]
        scores = jnp.where(valid, scores, MASKED)
        block_max = jnp.max(scores, axis=1, keepdims=True)
        expo = jnp.where(valid, jnp.exp(scores - block_max), 0.0)
        block_sum = jnp.sum(expo, axis=1, keepdims=True)
        full = jnp.dot(
            expo.astype(kv.dtype), kv[particle, 1], preferred_element_type=jnp.float32
        )
        acc = jnp.concatenate(
            [
                full[PAD_GROUP * g : PAD_GROUP * (g + 1), HD * g : HD * (g + 1)]
                for g in range(KVH)
            ],
            axis=0,
        )
        top = jnp.maximum(block_max, own_score)
        factor = jnp.exp(block_max - top)
        own_factor = jnp.where(first_device, jnp.exp(own_score - top), 0.0)
        acc = factor * acc + own_factor * own_value
        total = factor * block_sum + own_factor
        diagonal = eye()
        top_row = jnp.sum(jnp.where(diagonal, top, 0.0), axis=0, keepdims=True)
        total_row = jnp.sum(jnp.where(diagonal, total, 0.0), axis=0, keepdims=True)
        stats_row = lax.broadcasted_iota(jnp.int32, (8, HD), 0)
        stats = jnp.where(stats_row == 0, top_row, jnp.where(stats_row == 1, total_row, 0.0))
        for receiver in range(TP):
            out[receiver, PART * particle : PART * particle + ROWS, :] = acc
            out[receiver, PART * particle + ROWS : PART * (particle + 1), :] = stats


def attend(lengths, heads, new_kv, kept):
    return pl.pallas_call(
        attend_kernel,
        out_shape=jax.ShapeDtypeStruct((TP, P_DEV * PART, HD), jnp.float32),
        in_specs=[SMEM, VMEM, VMEM, VMEM],
        out_specs=VMEM,
        scratch_shapes=[pltpu.VMEM((ROWS, HD), jnp.float32)],
        compiler_params=pltpu.CompilerParams(vmem_limit_bytes=16 << 20),
        name="attend",
    )(lengths, heads, new_kv, kept)


def merge_kernel(prior, parts, weight, attn, logits, weights, all_rows, wide):
    tp_index = lax.axis_index("tp")
    for g in range(KVH):
        for half in range(2):
            at = PAD_GROUP * g + OWN * half
            head = GROUP * g + (OWN - 1) * half
            weights[at : at + OWN, :] = weight[head : head + OWN, :]
    in_group = lax.rem(lax.broadcasted_iota(jnp.int32, (ROWS, HD), 0), PAD_GROUP)
    lane = lax.broadcasted_iota(jnp.int32, (ROWS, HD), 1)
    counted = ((in_group != OWN - 1) | (lane < HD // 2)) & ((in_group != OWN) | (lane >= HD // 2))
    diagonal = eye()
    logit_lane = lax.broadcasted_iota(jnp.int32, (1, HD), 1)
    logit_row = jnp.zeros((1, HD), jnp.float32)
    wide[...] = jnp.zeros_like(wide)
    for particle in range(P_DEV):
        at = PART * particle
        tops, totals = [
            [
                jnp.sum(
                    jnp.where(diagonal, parts[source, at + ROWS + k : at + ROWS + k + 1, :], 0.0),
                    axis=1,
                    keepdims=True,
                )
                for source in range(TP)
            ]
            for k in range(2)
        ]
        top = functools.reduce(jnp.maximum, tops)
        denom = jnp.zeros_like(top)
        numer = jnp.zeros((ROWS, HD), jnp.float32)
        for source in range(TP):
            factor = jnp.exp(tops[source] - top)
            denom = denom + factor * totals[source]
            numer = numer + factor * parts[source, at : at + ROWS, :]
        attended = numer / denom
        kept = jnp.where(counted, attended, 0.0)
        mean = jnp.sum(kept * kept) / FEATURES
        weighed = jnp.sum(weights[...] * kept)
        reward = jnp.full((1, HD), weighed) / jnp.sqrt(jnp.full((1, HD), mean) + EPSILON)
        logit_row = jnp.where(logit_lane == particle, prior[particle] + reward, logit_row)
        all_rows[...] = attended
        for j in range(OWN):
            wide[particle : particle + 1, HD * j : HD * (j + 1)] = all_rows[
                pl.ds(OWN * tp_index + j, 1), :
            ]
    columns = attn.shape[1]
    even = wide[...]
    odd = pltpu.roll(even, columns, 1)
    chosen = jnp.where(lax.rem(tp_index, 2) == 1, odd, even)
    attn[...] = chosen[0:P_DEV, 0:columns].astype(attn.dtype)
    logits[...] = jnp.broadcast_to(logit_row[None], logits.shape)


def merge(prior, parts, weight, columns, devices):
    return pl.pallas_call(
        merge_kernel,
        out_shape=(
            jax.ShapeDtypeStruct((P_DEV, columns), jnp.bfloat16),
            jax.ShapeDtypeStruct((devices, 1, HD), jnp.float32),
        ),
        in_specs=[SMEM, VMEM, VMEM],
        out_specs=(VMEM, VMEM),
        scratch_shapes=[
            pltpu.VMEM((ROWS, HD), jnp.float32),
            pltpu.VMEM((ROWS, HD), jnp.float32),
            pltpu.VMEM((8, OWN * HD), jnp.float32),
        ],
        compiler_params=pltpu.CompilerParams(vmem_limit_bytes=8 << 20),
        cost_estimate=pl.CostEstimate(flops=10**11, bytes_accessed=10**9, transcendentals=0),
        name="merge",
    )(prior, parts, weight)


SPLIT = 2


def assemble_kernel(
    far, ancestors, lengths, new_kv, cache, even1, odd1, even2, odd2, new_cache, buffer, in_sems, out_sems
):
    device = lax.axis_index("dom")
    length = cache.shape[2]
    first = lax.axis_index("tp") * length
    rows = length // SPLIT
    pieces = [
        (slot, kv, part) for part in range(SPLIT) for kv in range(2) for slot in range(P_DEV)
    ]
    owner = [ancestors[P_DEV * device + slot] for slot in range(P_DEV)]

    def arriving(ref, piece):
        slot, kv, part = piece
        at = pl.ds(part * rows, rows)
        return pltpu.make_async_copy(ref.at[kv, at], buffer.at[slot, kv, at], in_sems.at[slot, kv, part])

    for piece in pieces:
        offset = (owner[piece[0]] >> 1) - device
        facing = offset * (1 - 2 * (device & 1))
        two = offset if far else facing

        @pl.when(offset == 0)
        def _():
            arriving(cache.at[owner[piece[0]] & 1], piece).start()

        for found, ref in (
            (facing == 1, even1),
            (facing == -1, odd1),
            (two == REACH, even2),
            (two == -REACH, odd2),
        ):

            @pl.when(found)
            def _():
                arriving(ref, piece).start()

    leaving = []
    for piece in pieces:
        slot, kv, part = piece
        at = pl.ds(part * rows, rows)
        arriving(even1, piece).wait()
        particle = owner[slot] & 1
        row = lengths[particle] - (first + part * rows)

        @pl.when((owner[slot] >> 1 == device) & (row >= 0) & (row < rows))
        def _():
            fresh = new_kv[particle].astype(jnp.float32)
            patch(buffer.at[slot, kv], 0, row + part * rows, fresh[kv : kv + 1])

        copy = pltpu.make_async_copy(
            buffer.at[slot, kv, at], new_cache.at[slot, kv, at], out_sems.at[slot, kv, part]
        )
        copy.start()
        leaving.append(copy)
    for copy in leaving:
        copy.wait()


def assemble(ancestors, lengths, new_kv, cache, even1, odd1, even2, odd2, far):
    return pl.pallas_call(
        functools.partial(assemble_kernel, far),
        out_shape=jax.ShapeDtypeStruct(cache.shape, cache.dtype),
        in_specs=[SMEM, SMEM, VMEM, ANY, ANY, ANY, ANY, ANY],
        out_specs=ANY,
        scratch_shapes=[
            pltpu.VMEM(cache.shape, cache.dtype),
            pltpu.SemaphoreType.DMA((P_DEV, 2, SPLIT)),
            pltpu.SemaphoreType.DMA((P_DEV, 2, SPLIT)),
        ],
        compiler_params=pltpu.CompilerParams(vmem_limit_bytes=16 << 20),
        name="assemble",
    )(ancestors, lengths, new_kv, cache, even1, odd1, even2, odd2)


def normalize_kernel(logits, log_weight):
    every = logits[...]
    every = jnp.where(lax.broadcasted_iota(jnp.int32, every.shape, 2) < P_DEV, every, -jnp.inf)
    peak = jnp.max(jnp.max(every, axis=0), axis=1, keepdims=True)
    total = jnp.sum(jnp.sum(jnp.exp(every - peak), axis=0), axis=1, keepdims=True)
    mine = logits[lax.axis_index("dom")] - (peak + jnp.log(total))
    for slot in range(P_DEV):
        log_weight[slot] = mine[0, slot]


def normalize(logits):
    return pl.pallas_call(
        normalize_kernel,
        out_shape=jax.ShapeDtypeStruct((P_DEV,), jnp.float32),
        in_specs=[VMEM],
        out_specs=SMEM,
        compiler_params=pltpu.CompilerParams(vmem_limit_bytes=8 << 20),
        name="normalize",
    )(logits)


def local(query, new_kv, cache, lengths, prior_logw, ancestors, w_reward):
    even0, odd0, rows, flag = pack(ancestors, lengths, query, new_kv, cache)
    even1 = swapped(even0, "dom", 0)
    odd1 = swapped(odd0, "dom", 1)
    heads = lax.all_to_all(rows, "tp", 0, 0)
    parts = attend(lengths, heads, new_kv, cache)
    weight = w_reward.astype(jnp.float32).reshape(HQ, HD)
    sent = parts
    parts = lax.all_to_all(parts, "tp", 0, 0)
    even1, sent = lax.optimization_barrier((even1, sent))
    odd2 = swapped(even1, "dom", 1)
    odd1, sent = lax.optimization_barrier((odd1, sent))
    even2 = swapped(odd1, "dom", 0)
    attn, logits = merge(prior_logw, parts, weight, query.shape[1], lax.axis_size("dom"))
    logits = lax.all_to_all(logits, "dom", 0, 0)

    def near(even2, odd2):
        return assemble(ancestors, lengths, new_kv, cache, even1, odd1, even2, odd2, far=False)

    def direct(even2, odd2):
        right0, left0 = pack_far(ancestors, lengths, new_kv, cache)
        from_left = shifted(right0, "dom", REACH)
        from_right = shifted(left0, "dom", -REACH)
        return assemble(
            ancestors, lengths, new_kv, cache, even1, odd1, from_right, from_left, far=True
        )

    new_cache = lax.cond(flag[0] > 0, direct, near, even2, odd2)
    new_cache, logits = lax.optimization_barrier((new_cache, logits))
    return (attn, normalize(logits), new_cache)


def solution(mesh):
    in_specs = (
        P("dom", "tp"),
        P("dom", None, None),
        P("dom", None, "tp", None),
        P("dom"),
        P("dom"),
        P(),
        P(),
    )
    out_specs = (P("dom", "tp"), P("dom"), P("dom", None, "tp", None))
    return jax.shard_map(local, mesh=mesh, in_specs=in_specs, out_specs=out_specs, check_vma=False)
```

```python
import functools

import jax
import jax.numpy as jnp
from jax import lax
from jax.experimental import pallas as pl
from jax.experimental.pallas import tpu as pltpu
from jax.sharding import PartitionSpec as P

HQ = 28
KVH = 4
HD = 128
GROUP = HQ // KVH
FEATURES = HQ * HD
REACH = 2
P_DEV = 2
TP = 8
ROWS = 32
OWN = ROWS // TP
PAD_GROUP = ROWS // KVH
PART = ROWS + 8
TILE = 16

MASKED = -1e30
EPSILON = 1e-06

ANY = pl.BlockSpec(memory_space=pl.ANY)
HBM = pl.BlockSpec(memory_space=pltpu.HBM)
SMEM = pl.BlockSpec(memory_space=pltpu.SMEM)
VMEM = pl.BlockSpec(memory_space=pltpu.VMEM)


def shifted(value, axis, by):
    devices = lax.axis_size(axis)
    pairs = [(i, i + by) for i in range(devices) if 0 <= i + by < devices]
    return lax.ppermute(value, axis, pairs)


def swapped(value, axis, first):
    pairs = []
    for i in range(first, lax.axis_size(axis) - 1, 2):
        pairs += [(i, i + 1), (i + 1, i)]
    return lax.ppermute(value, axis, pairs)


def patch(block, first_row, row, fresh):
    inside = row - first_row
    tile = pl.multiple_of((inside // TILE) * TILE, TILE)
    old = block[pl.ds(tile, TILE), :].astype(jnp.float32)
    here = lax.broadcasted_iota(jnp.int32, old.shape, 0) == inside - tile
    block[pl.ds(tile, TILE), :] = jnp.where(here, fresh, old).astype(block.dtype)


def pick(ancestors, device, receivers):
    count = ancestors.shape[0]
    chosen = jnp.int32(0)
    for receiver in reversed(receivers):
        for slot in range(P_DEV):
            lane = P_DEV * receiver + slot
            wanted = ancestors[jnp.clip(lane, 0, count - 1)]
            fits = (lane >= 0) & (lane < count) & (wanted >> 1 == device)
            chosen = jnp.where(fits, wanted & 1, chosen)
    return chosen


def crowded(ancestors):
    count = ancestors.shape[1]
    shape = (8, count)
    wanted = jnp.broadcast_to(ancestors[...], shape)
    lane = lax.broadcasted_iota(jnp.int32, shape, 1)
    offset = (wanted >> 1) - (lane >> 1)
    found = jnp.zeros(shape, jnp.float32)
    for ahead in range(1, 2 * P_DEV):
        later_wanted = pltpu.roll(wanted, count - ahead, 1)
        later_offset = pltpu.roll(offset, count - ahead, 1)
        differ = (wanted >> 1 == later_wanted >> 1) & (wanted != later_wanted)
        sides = ((offset == -1) & (later_offset == -2)) | ((offset == 2) & (later_offset == 1))
        found = jnp.where(differ & sides & (lane < count - ahead), 1.0, found)
    return (jnp.sum(found) > 0.0).astype(jnp.int32)


def spread_kernel(row, query, out, flag, wide):
    flag[0] = crowded(row)
    columns = query.shape[1]
    wide[...] = jnp.zeros_like(wide)
    wide[0:P_DEV, 0:columns] = query[...].astype(jnp.float32)
    even_rows = wide[...]
    odd_rows = pltpu.roll(even_rows, OWN * HD - columns, 1)
    rows = jnp.where(lax.rem(lax.axis_index("tp"), 2) == 1, odd_rows, even_rows)
    for particle in range(P_DEV):
        for j in range(OWN):
            one = rows[particle : particle + 1, HD * j : HD * (j + 1)]
            for receiver in range(TP):
                out[receiver, pl.ds(OWN * particle + j, 1), :] = one


def spread(ancestors, query):
    return pl.pallas_call(
        spread_kernel,
        out_shape=(
            jax.ShapeDtypeStruct((TP, P_DEV * OWN, HD), jnp.float32),
            jax.ShapeDtypeStruct((1,), jnp.int32),
        ),
        in_specs=[VMEM, VMEM],
        out_specs=(VMEM, SMEM),
        scratch_shapes=[pltpu.VMEM((8, OWN * HD), jnp.float32)],
        compiler_params=pltpu.CompilerParams(vmem_limit_bytes=8 << 20),
        name="spread",
    )(ancestors.reshape(1, -1), query)


def pack_kernel(far, ancestors, lengths, new_kv, cache, inner, outer, fresh, sems, small_sem):
    device = lax.axis_index("dom")
    length = cache.shape[2]
    first = lax.axis_index("tp") * length
    facing = 1 if far else 1 - 2 * (device & 1)
    units = []
    for side, (out, sign) in enumerate(((inner, facing), (outer, -facing))):
        receivers = [device + REACH * sign] if far else [device + sign, device + REACH * sign]
        particle = pick(ancestors, device, receivers)
        copy = pltpu.make_async_copy(cache.at[particle], out, sems.at[side])
        copy.start()
        units.append((out, particle, copy))
    small = pltpu.make_async_copy(new_kv, fresh, small_sem)
    small.start()
    small.wait()
    for out, particle, copy in units:
        copy.wait()
        position = lengths[particle]

        @pl.when((position >= first) & (position < first + length))
        def _():
            new = fresh[particle].astype(jnp.float32)
            for kv in range(2):
                patch(out.at[kv], first, position, new[kv : kv + 1])


def pack(ancestors, lengths, new_kv, cache, far):
    unit = jax.ShapeDtypeStruct(cache.shape[1:], cache.dtype)
    return pl.pallas_call(
        functools.partial(pack_kernel, far),
        out_shape=(unit, unit),
        in_specs=[SMEM, SMEM, HBM, HBM],
        out_specs=(VMEM, VMEM),
        scratch_shapes=[
            pltpu.VMEM(new_kv.shape, new_kv.dtype),
            pltpu.SemaphoreType.DMA((2,)),
            pltpu.SemaphoreType.DMA,
        ],
        compiler_params=pltpu.CompilerParams(vmem_limit_bytes=16 << 20),
        name="pack_far" if far else "pack",
    )(ancestors, lengths, new_kv, cache)


def eye():
    shape = (ROWS, HD)
    return lax.broadcasted_iota(jnp.int32, shape, 0) == lax.broadcasted_iota(jnp.int32, shape, 1)


def attend_kernel(lengths, heads, new_kv, kv, out, rows):
    length = kv.shape[2]
    tp_index = lax.axis_index("tp")
    scale = HD ** (-0.5)
    row_index = lax.broadcasted_iota(jnp.int32, (ROWS, HD), 0)
    in_group = lax.rem(row_index, PAD_GROUP)
    wide_shape = (ROWS, KVH * HD)
    own_block = (
        lax.broadcasted_iota(jnp.int32, wide_shape, 0) // PAD_GROUP
        == lax.broadcasted_iota(jnp.int32, wide_shape, 1) // HD
    )
    for particle in range(P_DEV):
        for source in range(TP):
            rows[OWN * source : OWN * (source + 1), :] = heads[
                source, OWN * particle : OWN * (particle + 1), :
            ]
        parts = rows[...]
        after = pltpu.roll(parts, ROWS - 1, 0)
        before = pltpu.roll(parts, 1, 0)
        query = (
            parts
            + jnp.where(in_group == OWN - 1, after, 0.0)
            + jnp.where(in_group == OWN, before, 0.0)
        )
        fresh = new_kv[particle].astype(jnp.float32)
        own_key, own_value = [
            jnp.concatenate(
                [
                    jnp.broadcast_to(fresh[half : half + 1, HD * g : HD * (g + 1)], (PAD_GROUP, HD))
                    for g in range(KVH)
                ],
                axis=0,
            )
            for half in range(2)
        ]
        first_device = tp_index == 0
        own_score = jnp.sum(query * own_key, axis=1, keepdims=True) * scale
        own_score = jnp.where(first_device, own_score, MASKED)
        wide = jnp.concatenate([query] * KVH, axis=1)
        wide = jnp.where(own_block, wide, 0.0).astype(kv.dtype)
        scores = (
            lax.dot_general(
                wide, kv[particle, 0], (((1,), (1,)), ((), ())), preferred_element_type=jnp.float32
            )
            * scale
        )
        position = tp_index * length + lax.broadcasted_iota(jnp.int32, scores.shape, 1)
        valid = position < lengths[particle]
        scores = jnp.where(valid, scores, MASKED)
        block_max = jnp.max(scores, axis=1, keepdims=True)
        expo = jnp.where(valid, jnp.exp(scores - block_max), 0.0)
        block_sum = jnp.sum(expo, axis=1, keepdims=True)
        full = jnp.dot(
            expo.astype(kv.dtype), kv[particle, 1], preferred_element_type=jnp.float32
        )
        acc = jnp.concatenate(
            [
                full[PAD_GROUP * g : PAD_GROUP * (g + 1), HD * g : HD * (g + 1)]
                for g in range(KVH)
            ],
            axis=0,
        )
        top = jnp.maximum(block_max, own_score)
        factor = jnp.exp(block_max - top)
        own_factor = jnp.where(first_device, jnp.exp(own_score - top), 0.0)
        acc = factor * acc + own_factor * own_value
        total = factor * block_sum + own_factor
        diagonal = eye()
        top_row = jnp.sum(jnp.where(diagonal, top, 0.0), axis=0, keepdims=True)
        total_row = jnp.sum(jnp.where(diagonal, total, 0.0), axis=0, keepdims=True)
        stats_row = lax.broadcasted_iota(jnp.int32, (8, HD), 0)
        stats = jnp.where(stats_row == 0, top_row, jnp.where(stats_row == 1, total_row, 0.0))
        for receiver in range(TP):
            out[receiver, PART * particle : PART * particle + ROWS, :] = acc
            out[receiver, PART * particle + ROWS : PART * (particle + 1), :] = stats


def attend(lengths, heads, new_kv, kept):
    return pl.pallas_call(
        attend_kernel,
        out_shape=jax.ShapeDtypeStruct((TP, P_DEV * PART, HD), jnp.float32),
        in_specs=[SMEM, VMEM, VMEM, VMEM],
        out_specs=VMEM,
        scratch_shapes=[pltpu.VMEM((ROWS, HD), jnp.float32)],
        compiler_params=pltpu.CompilerParams(vmem_limit_bytes=16 << 20),
        name="attend",
    )(lengths, heads, new_kv, kept)


def merge_kernel(prior, parts, weight, attn, logits, weights, all_rows, wide):
    tp_index = lax.axis_index("tp")
    for g in range(KVH):
        for half in range(2):
            at = PAD_GROUP * g + OWN * half
            head = GROUP * g + (OWN - 1) * half
            weights[at : at + OWN, :] = weight[head : head + OWN, :]
    in_group = lax.rem(lax.broadcasted_iota(jnp.int32, (ROWS, HD), 0), PAD_GROUP)
    lane = lax.broadcasted_iota(jnp.int32, (ROWS, HD), 1)
    counted = ((in_group != OWN - 1) | (lane < HD // 2)) & ((in_group != OWN) | (lane >= HD // 2))
    diagonal = eye()
    logit_lane = lax.broadcasted_iota(jnp.int32, (1, HD), 1)
    logit_row = jnp.zeros((1, HD), jnp.float32)
    wide[...] = jnp.zeros_like(wide)
    for particle in range(P_DEV):
        at = PART * particle
        tops, totals = [
            [
                jnp.sum(
                    jnp.where(diagonal, parts[source, at + ROWS + k : at + ROWS + k + 1, :], 0.0),
                    axis=1,
                    keepdims=True,
                )
                for source in range(TP)
            ]
            for k in range(2)
        ]
        top = functools.reduce(jnp.maximum, tops)
        denom = jnp.zeros_like(top)
        numer = jnp.zeros((ROWS, HD), jnp.float32)
        for source in range(TP):
            factor = jnp.exp(tops[source] - top)
            denom = denom + factor * totals[source]
            numer = numer + factor * parts[source, at : at + ROWS, :]
        attended = numer / denom
        kept = jnp.where(counted, attended, 0.0)
        mean = jnp.sum(kept * kept) / FEATURES
        weighed = jnp.sum(weights[...] * kept)
        reward = jnp.full((1, HD), weighed) / jnp.sqrt(jnp.full((1, HD), mean) + EPSILON)
        logit_row = jnp.where(logit_lane == particle, prior[particle] + reward, logit_row)
        all_rows[...] = attended
        for j in range(OWN):
            wide[particle : particle + 1, HD * j : HD * (j + 1)] = all_rows[
                pl.ds(OWN * tp_index + j, 1), :
            ]
    columns = attn.shape[1]
    even = wide[...]
    odd = pltpu.roll(even, columns, 1)
    chosen = jnp.where(lax.rem(tp_index, 2) == 1, odd, even)
    attn[...] = chosen[0:P_DEV, 0:columns].astype(attn.dtype)
    logits[...] = jnp.broadcast_to(logit_row[None], logits.shape)


def merge(prior, parts, weight, columns, devices):
    return pl.pallas_call(
        merge_kernel,
        out_shape=(
            jax.ShapeDtypeStruct((P_DEV, columns), jnp.bfloat16),
            jax.ShapeDtypeStruct((devices, 1, HD), jnp.float32),
        ),
        in_specs=[SMEM, VMEM, VMEM],
        out_specs=(VMEM, VMEM),
        scratch_shapes=[
            pltpu.VMEM((ROWS, HD), jnp.float32),
            pltpu.VMEM((ROWS, HD), jnp.float32),
            pltpu.VMEM((8, OWN * HD), jnp.float32),
        ],
        compiler_params=pltpu.CompilerParams(vmem_limit_bytes=8 << 20),
        cost_estimate=pl.CostEstimate(flops=10**11, bytes_accessed=10**9, transcendentals=0),
        name="merge",
    )(prior, parts, weight)


def assemble_kernel(
    ancestors, lengths, new_kv, cache, inner1, outer1, new_cache, buffer, in_sems, out_sems
):
    device = lax.axis_index("dom")
    length = cache.shape[2]
    first = lax.axis_index("tp") * length

    def enter(ref, slot, kv):
        return pltpu.make_async_copy(ref.at[kv], buffer.at[slot, kv], in_sems.at[slot, kv])

    def leave(slot, kv):
        return pltpu.make_async_copy(
            buffer.at[slot, kv], new_cache.at[slot, kv], out_sems.at[slot, kv]
        )

    slots = []
    for slot in range(P_DEV):
        owner = ancestors[P_DEV * device + slot]
        particle = owner & 1
        offset = (owner >> 1) - device
        facing = offset * (1 - 2 * (device & 1))
        for found, ref in ((offset == 0, cache.at[particle]), (facing == 1, inner1), (facing == -1, outer1)):

            @pl.when(found)
            def _():
                for kv in range(2):
                    enter(ref, slot, kv).start()

        row = lengths[particle]
        patched = (offset == 0) & (row >= first) & (row < first + length)
        slots.append((slot, particle, row, patched, jnp.abs(offset) <= 1))
    for slot, particle, row, patched, near in slots:
        for kv in range(2):

            @pl.when(near)
            def _():
                enter(inner1, slot, kv).wait()

            @pl.when(patched)
            def _():
                fresh = new_kv[particle].astype(jnp.float32)
                patch(buffer.at[slot, kv], first, row, fresh[kv : kv + 1])

            @pl.when(near)
            def _():
                leave(slot, kv).start()

    for slot, particle, row, patched, near in slots:
        for kv in range(2):

            @pl.when(near)
            def _():
                leave(slot, kv).wait()


def finish_kernel(far, ancestors, inner2, outer2, held, new_cache, sems):
    device = lax.axis_index("dom")
    slots = []
    for slot in range(P_DEV):
        offset = (ancestors[P_DEV * device + slot] >> 1) - device
        side = offset if far else offset * (1 - 2 * (device & 1))
        for found, ref in ((side == REACH, inner2), (side == -REACH, outer2)):

            @pl.when(found)
            def _():
                pltpu.make_async_copy(ref, new_cache.at[slot], sems.at[slot]).start()

        slots.append((slot, jnp.abs(offset) == REACH))
    for slot, found in slots:

        @pl.when(found)
        def _():
            pltpu.make_async_copy(outer2, new_cache.at[slot], sems.at[slot]).wait()


def assemble(ancestors, lengths, new_kv, cache, inner1, outer1):
    return pl.pallas_call(
        assemble_kernel,
        out_shape=jax.ShapeDtypeStruct(cache.shape, cache.dtype),
        in_specs=[SMEM, SMEM, VMEM, ANY, ANY, ANY],
        out_specs=HBM,
        scratch_shapes=[
            pltpu.VMEM(cache.shape, cache.dtype),
            pltpu.SemaphoreType.DMA((P_DEV, 2)),
            pltpu.SemaphoreType.DMA((P_DEV, 2)),
        ],
        compiler_params=pltpu.CompilerParams(vmem_limit_bytes=16 << 20),
        name="assemble",
    )(ancestors, lengths, new_kv, cache, inner1, outer1)


def finish(ancestors, inner2, outer2, new_cache, far):
    return pl.pallas_call(
        functools.partial(finish_kernel, far),
        out_shape=jax.ShapeDtypeStruct(new_cache.shape, new_cache.dtype),
        in_specs=[SMEM, VMEM, VMEM, HBM],
        out_specs=HBM,
        input_output_aliases={3: 0},
        scratch_shapes=[pltpu.SemaphoreType.DMA((P_DEV,))],
        compiler_params=pltpu.CompilerParams(vmem_limit_bytes=16 << 20),
        name="finish",
    )(ancestors, inner2, outer2, new_cache)


def normalize_kernel(logits, log_weight):
    every = logits[...]
    every = jnp.where(lax.broadcasted_iota(jnp.int32, every.shape, 2) < P_DEV, every, -jnp.inf)
    peak = jnp.max(jnp.max(every, axis=0), axis=1, keepdims=True)
    total = jnp.sum(jnp.sum(jnp.exp(every - peak), axis=0), axis=1, keepdims=True)
    mine = logits[lax.axis_index("dom")] - (peak + jnp.log(total))
    for slot in range(P_DEV):
        log_weight[slot] = mine[0, slot]


def normalize(logits):
    return pl.pallas_call(
        normalize_kernel,
        out_shape=jax.ShapeDtypeStruct((P_DEV,), jnp.float32),
        in_specs=[VMEM],
        out_specs=SMEM,
        compiler_params=pltpu.CompilerParams(vmem_limit_bytes=8 << 20),
        name="normalize",
    )(logits)


def local(query, new_kv, cache, lengths, prior_logw, ancestors, w_reward):
    inner0, outer0 = pack(ancestors, lengths, new_kv, cache, far=False)
    inner1 = swapped(inner0, "dom", 0)
    outer1 = swapped(outer0, "dom", 1)
    query, outer0 = lax.optimization_barrier((query, outer0))
    rows, flag = spread(ancestors, query)
    heads = lax.all_to_all(rows, "tp", 0, 0)
    heads, flag = lax.optimization_barrier((heads, flag))
    parts = attend(lengths, heads, new_kv, cache)
    weight = w_reward.astype(jnp.float32).reshape(HQ, HD)
    sent = parts
    parts = lax.all_to_all(parts, "tp", 0, 0)
    inner1, sent = lax.optimization_barrier((inner1, sent))
    outer2 = swapped(inner1, "dom", 1)
    outer1, sent = lax.optimization_barrier((outer1, sent))
    inner2 = swapped(outer1, "dom", 0)
    attn, logits = merge(prior_logw, parts, weight, query.shape[1], lax.axis_size("dom"))
    logits, held_ancestors = lax.optimization_barrier((logits, ancestors))
    logits = lax.all_to_all(logits, "dom", 0, 0)
    new_cache = assemble(held_ancestors, lengths, new_kv, cache, inner1, outer1)

    new_cache = finish(ancestors, inner2, outer2, new_cache, far=False)

    def direct(new_cache):
        right0, left0 = pack(ancestors, lengths, new_kv, cache, far=True)
        from_left = shifted(right0, "dom", REACH)
        from_right = shifted(left0, "dom", -REACH)
        return finish(ancestors, from_right, from_left, new_cache, far=True)

    new_cache = lax.cond(flag[0] > 0, direct, lambda new_cache: new_cache, new_cache)
    new_cache, logits = lax.optimization_barrier((new_cache, logits))
    return (attn, normalize(logits), new_cache)


def solution(mesh):
    in_specs = (
        P("dom", "tp"),
        P("dom", None, None),
        P("dom", None, "tp", None),
        P("dom"),
        P("dom"),
        P(),
        P(),
    )
    out_specs = (P("dom", "tp"), P("dom"), P("dom", None, "tp", None))
    return jax.shard_map(local, mesh=mesh, in_specs=in_specs, out_specs=out_specs, check_vma=False)
```

```python
import functools

import jax
import jax.numpy as jnp
from jax import lax
from jax.experimental import pallas as pl
from jax.experimental.pallas import tpu as pltpu
from jax.sharding import PartitionSpec as P

HQ = 28
KVH = 4
HD = 128
GROUP = HQ // KVH
FEATURES = HQ * HD
REACH = 2
P_DEV = 2
TP = 8
ROWS = 32
OWN = ROWS // TP
PAD_GROUP = ROWS // KVH
PART = ROWS + 8
TILE = 16

MASKED = -1e30
EPSILON = 1e-06

ANY = pl.BlockSpec(memory_space=pl.ANY)
HBM = pl.BlockSpec(memory_space=pltpu.HBM)
SMEM = pl.BlockSpec(memory_space=pltpu.SMEM)
VMEM = pl.BlockSpec(memory_space=pltpu.VMEM)


def shifted(value, axis, by):
    devices = lax.axis_size(axis)
    pairs = [(i, i + by) for i in range(devices) if 0 <= i + by < devices]
    return lax.ppermute(value, axis, pairs)


def swapped(value, axis, first):
    pairs = []
    for i in range(first, lax.axis_size(axis) - 1, 2):
        pairs += [(i, i + 1), (i + 1, i)]
    return lax.ppermute(value, axis, pairs)


def patch(block, first_row, row, fresh):
    inside = row - first_row
    tile = pl.multiple_of((inside // TILE) * TILE, TILE)
    old = block[pl.ds(tile, TILE), :].astype(jnp.float32)
    here = lax.broadcasted_iota(jnp.int32, old.shape, 0) == inside - tile
    block[pl.ds(tile, TILE), :] = jnp.where(here, fresh, old).astype(block.dtype)


def pick(ancestors, device, receivers):
    count = ancestors.shape[0]
    chosen = jnp.int32(0)
    for receiver in reversed(receivers):
        for slot in range(P_DEV):
            lane = P_DEV * receiver + slot
            wanted = ancestors[jnp.clip(lane, 0, count - 1)]
            fits = (lane >= 0) & (lane < count) & (wanted >> 1 == device)
            chosen = jnp.where(fits, wanted & 1, chosen)
    return chosen


def crowded(ancestors):
    count = ancestors.shape[1]
    shape = (8, count)
    wanted = jnp.broadcast_to(ancestors[...], shape)
    lane = lax.broadcasted_iota(jnp.int32, shape, 1)
    offset = (wanted >> 1) - (lane >> 1)
    found = jnp.zeros(shape, jnp.float32)
    for ahead in range(1, 2 * P_DEV):
        later_wanted = pltpu.roll(wanted, count - ahead, 1)
        later_offset = pltpu.roll(offset, count - ahead, 1)
        differ = (wanted >> 1 == later_wanted >> 1) & (wanted != later_wanted)
        sides = ((offset == -1) & (later_offset == -2)) | ((offset == 2) & (later_offset == 1))
        found = jnp.where(differ & sides & (lane < count - ahead), 1.0, found)
    return (jnp.sum(found) > 0.0).astype(jnp.int32)


def spread_kernel(row, query, out, flag, wide):
    flag[0] = crowded(row)
    columns = query.shape[1]
    wide[...] = jnp.zeros_like(wide)
    wide[0:P_DEV, 0:columns] = query[...].astype(jnp.float32)
    even_rows = wide[...]
    odd_rows = pltpu.roll(even_rows, OWN * HD - columns, 1)
    rows = jnp.where(lax.rem(lax.axis_index("tp"), 2) == 1, odd_rows, even_rows)
    for particle in range(P_DEV):
        for j in range(OWN):
            one = rows[particle : particle + 1, HD * j : HD * (j + 1)]
            for receiver in range(TP):
                out[receiver, pl.ds(OWN * particle + j, 1), :] = one


def spread(ancestors, query):
    return pl.pallas_call(
        spread_kernel,
        out_shape=(
            jax.ShapeDtypeStruct((TP, P_DEV * OWN, HD), jnp.float32),
            jax.ShapeDtypeStruct((1,), jnp.int32),
        ),
        in_specs=[VMEM, VMEM],
        out_specs=(VMEM, SMEM),
        scratch_shapes=[pltpu.VMEM((8, OWN * HD), jnp.float32)],
        compiler_params=pltpu.CompilerParams(vmem_limit_bytes=8 << 20),
        name="spread",
    )(ancestors.reshape(1, -1), query)


def pack_kernel(far, ancestors, lengths, new_kv, cache, inner, outer, fresh, sems, small_sem):
    device = lax.axis_index("dom")
    length = cache.shape[2]
    first = lax.axis_index("tp") * length
    facing = 1 if far else 1 - 2 * (device & 1)
    units = []
    for side, (out, sign) in enumerate(((inner, facing), (outer, -facing))):
        receivers = [device + REACH * sign] if far else [device + sign, device + REACH * sign]
        particle = pick(ancestors, device, receivers)
        copy = pltpu.make_async_copy(cache.at[particle], out, sems.at[side])
        copy.start()
        units.append((out, particle, copy))
    small = pltpu.make_async_copy(new_kv, fresh, small_sem)
    small.start()
    small.wait()
    for out, particle, copy in units:
        copy.wait()
        position = lengths[particle]

        @pl.when((position >= first) & (position < first + length))
        def _():
            new = fresh[particle].astype(jnp.float32)
            for kv in range(2):
                patch(out.at[kv], first, position, new[kv : kv + 1])


def pack(ancestors, lengths, new_kv, cache, far):
    unit = jax.ShapeDtypeStruct(cache.shape[1:], cache.dtype)
    return pl.pallas_call(
        functools.partial(pack_kernel, far),
        out_shape=(unit, unit),
        in_specs=[SMEM, SMEM, HBM, HBM],
        out_specs=(VMEM, VMEM),
        scratch_shapes=[
            pltpu.VMEM(new_kv.shape, new_kv.dtype),
            pltpu.SemaphoreType.DMA((2,)),
            pltpu.SemaphoreType.DMA,
        ],
        compiler_params=pltpu.CompilerParams(vmem_limit_bytes=16 << 20),
        name="pack_far" if far else "pack",
    )(ancestors, lengths, new_kv, cache)


def eye():
    shape = (ROWS, HD)
    return lax.broadcasted_iota(jnp.int32, shape, 0) == lax.broadcasted_iota(jnp.int32, shape, 1)


def attend_kernel(lengths, heads, new_kv, kv, out, rows):
    length = kv.shape[2]
    tp_index = lax.axis_index("tp")
    scale = HD ** (-0.5)
    row_index = lax.broadcasted_iota(jnp.int32, (ROWS, HD), 0)
    in_group = lax.rem(row_index, PAD_GROUP)
    wide_shape = (ROWS, KVH * HD)
    own_block = (
        lax.broadcasted_iota(jnp.int32, wide_shape, 0) // PAD_GROUP
        == lax.broadcasted_iota(jnp.int32, wide_shape, 1) // HD
    )
    for particle in range(P_DEV):
        for source in range(TP):
            rows[OWN * source : OWN * (source + 1), :] = heads[
                source, OWN * particle : OWN * (particle + 1), :
            ]
        parts = rows[...]
        after = pltpu.roll(parts, ROWS - 1, 0)
        before = pltpu.roll(parts, 1, 0)
        query = (
            parts
            + jnp.where(in_group == OWN - 1, after, 0.0)
            + jnp.where(in_group == OWN, before, 0.0)
        )
        fresh = new_kv[particle].astype(jnp.float32)
        own_key, own_value = [
            jnp.concatenate(
                [
                    jnp.broadcast_to(fresh[half : half + 1, HD * g : HD * (g + 1)], (PAD_GROUP, HD))
                    for g in range(KVH)
                ],
                axis=0,
            )
            for half in range(2)
        ]
        first_device = tp_index == 0
        own_score = jnp.sum(query * own_key, axis=1, keepdims=True) * scale
        own_score = jnp.where(first_device, own_score, MASKED)
        wide = jnp.concatenate([query] * KVH, axis=1)
        wide = jnp.where(own_block, wide, 0.0).astype(kv.dtype)
        scores = (
            lax.dot_general(
                wide, kv[particle, 0], (((1,), (1,)), ((), ())), preferred_element_type=jnp.float32
            )
            * scale
        )
        position = tp_index * length + lax.broadcasted_iota(jnp.int32, scores.shape, 1)
        valid = position < lengths[particle]
        scores = jnp.where(valid, scores, MASKED)
        block_max = jnp.max(scores, axis=1, keepdims=True)
        expo = jnp.where(valid, jnp.exp(scores - block_max), 0.0)
        block_sum = jnp.sum(expo, axis=1, keepdims=True)
        full = jnp.dot(
            expo.astype(kv.dtype), kv[particle, 1], preferred_element_type=jnp.float32
        )
        acc = jnp.concatenate(
            [
                full[PAD_GROUP * g : PAD_GROUP * (g + 1), HD * g : HD * (g + 1)]
                for g in range(KVH)
            ],
            axis=0,
        )
        top = jnp.maximum(block_max, own_score)
        factor = jnp.exp(block_max - top)
        own_factor = jnp.where(first_device, jnp.exp(own_score - top), 0.0)
        acc = factor * acc + own_factor * own_value
        total = factor * block_sum + own_factor
        diagonal = eye()
        top_row = jnp.sum(jnp.where(diagonal, top, 0.0), axis=0, keepdims=True)
        total_row = jnp.sum(jnp.where(diagonal, total, 0.0), axis=0, keepdims=True)
        stats_row = lax.broadcasted_iota(jnp.int32, (8, HD), 0)
        stats = jnp.where(stats_row == 0, top_row, jnp.where(stats_row == 1, total_row, 0.0))
        for receiver in range(TP):
            out[receiver, PART * particle : PART * particle + ROWS, :] = acc
            out[receiver, PART * particle + ROWS : PART * (particle + 1), :] = stats


def attend(lengths, heads, new_kv, kept):
    return pl.pallas_call(
        attend_kernel,
        out_shape=jax.ShapeDtypeStruct((TP, P_DEV * PART, HD), jnp.float32),
        in_specs=[SMEM, VMEM, VMEM, VMEM],
        out_specs=VMEM,
        scratch_shapes=[pltpu.VMEM((ROWS, HD), jnp.float32)],
        compiler_params=pltpu.CompilerParams(vmem_limit_bytes=16 << 20),
        name="attend",
    )(lengths, heads, new_kv, kept)


def merge_kernel(prior, parts, weight, attn, logits, weights, all_rows, wide):
    tp_index = lax.axis_index("tp")
    for g in range(KVH):
        for half in range(2):
            at = PAD_GROUP * g + OWN * half
            head = GROUP * g + (OWN - 1) * half
            weights[at : at + OWN, :] = weight[head : head + OWN, :]
    in_group = lax.rem(lax.broadcasted_iota(jnp.int32, (ROWS, HD), 0), PAD_GROUP)
    lane = lax.broadcasted_iota(jnp.int32, (ROWS, HD), 1)
    counted = ((in_group != OWN - 1) | (lane < HD // 2)) & ((in_group != OWN) | (lane >= HD // 2))
    diagonal = eye()
    logit_lane = lax.broadcasted_iota(jnp.int32, (1, HD), 1)
    logit_row = jnp.zeros((1, HD), jnp.float32)
    wide[...] = jnp.zeros_like(wide)
    for particle in range(P_DEV):
        at = PART * particle
        tops, totals = [
            [
                jnp.sum(
                    jnp.where(diagonal, parts[source, at + ROWS + k : at + ROWS + k + 1, :], 0.0),
                    axis=1,
                    keepdims=True,
                )
                for source in range(TP)
            ]
            for k in range(2)
        ]
        top = functools.reduce(jnp.maximum, tops)
        denom = jnp.zeros_like(top)
        numer = jnp.zeros((ROWS, HD), jnp.float32)
        for source in range(TP):
            factor = jnp.exp(tops[source] - top)
            denom = denom + factor * totals[source]
            numer = numer + factor * parts[source, at : at + ROWS, :]
        attended = numer / denom
        kept = jnp.where(counted, attended, 0.0)
        mean = jnp.sum(kept * kept) / FEATURES
        weighed = jnp.sum(weights[...] * kept)
        reward = jnp.full((1, HD), weighed) / jnp.sqrt(jnp.full((1, HD), mean) + EPSILON)
        logit_row = jnp.where(logit_lane == particle, prior[particle] + reward, logit_row)
        all_rows[...] = attended
        for j in range(OWN):
            wide[particle : particle + 1, HD * j : HD * (j + 1)] = all_rows[
                pl.ds(OWN * tp_index + j, 1), :
            ]
    columns = attn.shape[1]
    even = wide[...]
    odd = pltpu.roll(even, columns, 1)
    chosen = jnp.where(lax.rem(tp_index, 2) == 1, odd, even)
    attn[...] = chosen[0:P_DEV, 0:columns].astype(attn.dtype)
    logits[...] = jnp.broadcast_to(logit_row[None], logits.shape)


def merge(prior, parts, weight, columns, devices):
    return pl.pallas_call(
        merge_kernel,
        out_shape=(
            jax.ShapeDtypeStruct((P_DEV, columns), jnp.bfloat16),
            jax.ShapeDtypeStruct((devices, 1, HD), jnp.float32),
        ),
        in_specs=[SMEM, VMEM, VMEM],
        out_specs=(VMEM, VMEM),
        scratch_shapes=[
            pltpu.VMEM((ROWS, HD), jnp.float32),
            pltpu.VMEM((ROWS, HD), jnp.float32),
            pltpu.VMEM((8, OWN * HD), jnp.float32),
        ],
        compiler_params=pltpu.CompilerParams(vmem_limit_bytes=8 << 20),
        name="merge",
    )(prior, parts, weight)


def assemble_kernel(
    ancestors, lengths, new_kv, cache, inner1, outer1, new_cache, buffer, in_sems, out_sems
):
    device = lax.axis_index("dom")
    length = cache.shape[2]
    first = lax.axis_index("tp") * length

    def enter(ref, slot, kv):
        return pltpu.make_async_copy(ref.at[kv], buffer.at[slot, kv], in_sems.at[slot, kv])

    def leave(slot, kv):
        return pltpu.make_async_copy(
            buffer.at[slot, kv], new_cache.at[slot, kv], out_sems.at[slot, kv]
        )

    slots = []
    for slot in range(P_DEV):
        owner = ancestors[P_DEV * device + slot]
        particle = owner & 1
        offset = (owner >> 1) - device
        facing = offset * (1 - 2 * (device & 1))
        for found, ref in ((offset == 0, cache.at[particle]), (facing == 1, inner1), (facing == -1, outer1)):

            @pl.when(found)
            def _():
                for kv in range(2):
                    enter(ref, slot, kv).start()

        row = lengths[particle]
        patched = (offset == 0) & (row >= first) & (row < first + length)
        slots.append((slot, particle, row, patched, jnp.abs(offset) <= 1))
    for slot, particle, row, patched, near in slots:
        for kv in range(2):

            @pl.when(near)
            def _():
                enter(inner1, slot, kv).wait()

            @pl.when(patched)
            def _():
                fresh = new_kv[particle].astype(jnp.float32)
                patch(buffer.at[slot, kv], first, row, fresh[kv : kv + 1])

            @pl.when(near)
            def _():
                leave(slot, kv).start()

    for slot, particle, row, patched, near in slots:
        for kv in range(2):

            @pl.when(near)
            def _():
                leave(slot, kv).wait()


def finish_kernel(far, ancestors, inner2, outer2, held, new_cache, sems):
    device = lax.axis_index("dom")
    slots = []
    for slot in range(P_DEV):
        offset = (ancestors[P_DEV * device + slot] >> 1) - device
        side = offset if far else offset * (1 - 2 * (device & 1))
        for found, ref in ((side == REACH, inner2), (side == -REACH, outer2)):

            @pl.when(found)
            def _():
                pltpu.make_async_copy(ref, new_cache.at[slot], sems.at[slot]).start()

        slots.append((slot, jnp.abs(offset) == REACH))
    for slot, found in slots:

        @pl.when(found)
        def _():
            pltpu.make_async_copy(outer2, new_cache.at[slot], sems.at[slot]).wait()


def assemble(ancestors, lengths, new_kv, cache, inner1, outer1):
    return pl.pallas_call(
        assemble_kernel,
        out_shape=jax.ShapeDtypeStruct(cache.shape, cache.dtype),
        in_specs=[SMEM, SMEM, VMEM, ANY, ANY, ANY],
        out_specs=HBM,
        scratch_shapes=[
            pltpu.VMEM(cache.shape, cache.dtype),
            pltpu.SemaphoreType.DMA((P_DEV, 2)),
            pltpu.SemaphoreType.DMA((P_DEV, 2)),
        ],
        compiler_params=pltpu.CompilerParams(vmem_limit_bytes=16 << 20),
        name="assemble",
    )(ancestors, lengths, new_kv, cache, inner1, outer1)


def finish(ancestors, inner2, outer2, new_cache, far):
    return pl.pallas_call(
        functools.partial(finish_kernel, far),
        out_shape=jax.ShapeDtypeStruct(new_cache.shape, new_cache.dtype),
        in_specs=[SMEM, VMEM, VMEM, HBM],
        out_specs=HBM,
        input_output_aliases={3: 0},
        scratch_shapes=[pltpu.SemaphoreType.DMA((P_DEV,))],
        compiler_params=pltpu.CompilerParams(vmem_limit_bytes=16 << 20),
        name="finish",
    )(ancestors, inner2, outer2, new_cache)


def normalize_kernel(logits, log_weight):
    every = logits[...]
    every = jnp.where(lax.broadcasted_iota(jnp.int32, every.shape, 2) < P_DEV, every, -jnp.inf)
    peak = jnp.max(jnp.max(every, axis=0), axis=1, keepdims=True)
    total = jnp.sum(jnp.sum(jnp.exp(every - peak), axis=0), axis=1, keepdims=True)
    mine = logits[lax.axis_index("dom")] - (peak + jnp.log(total))
    for slot in range(P_DEV):
        log_weight[slot] = mine[0, slot]


def normalize(logits):
    return pl.pallas_call(
        normalize_kernel,
        out_shape=jax.ShapeDtypeStruct((P_DEV,), jnp.float32),
        in_specs=[VMEM],
        out_specs=SMEM,
        compiler_params=pltpu.CompilerParams(vmem_limit_bytes=8 << 20),
        name="normalize",
    )(logits)


def local(query, new_kv, cache, lengths, prior_logw, ancestors, w_reward):
    inner0, outer0 = pack(ancestors, lengths, new_kv, cache, far=False)
    inner1 = swapped(inner0, "dom", 0)
    outer1 = swapped(outer0, "dom", 1)
    query, outer0 = lax.optimization_barrier((query, outer0))
    rows, flag = spread(ancestors, query)
    heads = lax.all_to_all(rows, "tp", 0, 0)
    heads, flag = lax.optimization_barrier((heads, flag))
    parts = attend(lengths, heads, new_kv, cache)
    weight = w_reward.astype(jnp.float32).reshape(HQ, HD)
    parts = lax.all_to_all(parts, "tp", 0, 0)
    attn, logits = merge(prior_logw, parts, weight, query.shape[1], lax.axis_size("dom"))
    inner1, logits = lax.optimization_barrier((inner1, logits))
    outer2 = swapped(inner1, "dom", 1)
    outer1, logits = lax.optimization_barrier((outer1, logits))
    inner2 = swapped(outer1, "dom", 0)
    logits, held_ancestors = lax.optimization_barrier((logits, ancestors))
    logits = lax.all_to_all(logits, "dom", 0, 0)
    new_cache = assemble(held_ancestors, lengths, new_kv, cache, inner1, outer1)

    new_cache = finish(ancestors, inner2, outer2, new_cache, far=False)

    def direct(new_cache):
        right0, left0 = pack(ancestors, lengths, new_kv, cache, far=True)
        from_left = shifted(right0, "dom", REACH)
        from_right = shifted(left0, "dom", -REACH)
        return finish(ancestors, from_right, from_left, new_cache, far=True)

    new_cache = lax.cond(flag[0] > 0, direct, lambda new_cache: new_cache, new_cache)
    new_cache, logits = lax.optimization_barrier((new_cache, logits))
    return (attn, normalize(logits), new_cache)


def solution(mesh):
    in_specs = (
        P("dom", "tp"),
        P("dom", None, None),
        P("dom", None, "tp", None),
        P("dom"),
        P("dom"),
        P(),
        P(),
    )
    out_specs = (P("dom", "tp"), P("dom"), P("dom", None, "tp", None))
    return jax.shard_map(local, mesh=mesh, in_specs=in_specs, out_specs=out_specs, check_vma=False)
```
